128 devices in a mesh: cube: 128 (over y, z, x, core).
Axes of the slice: x: 4, y: 4, z: 4, core: 2. Of those that a mesh axis runs over, the one named last changes fastest.
Arguments:
- front_leaf: bfloat16 [2048, 16384], P(None, 'cube'), may hold values from -6 to 6
- front_lower: bfloat16 [4096, 16384], P(None, 'cube'), may hold values from -6 to 6
- front_upper: bfloat16 [8192, 16384], P(None, 'cube'), may hold values from -6 to 6
- front_root: bfloat16 [16384, 16384], P(None, 'cube'), may hold values from -6 to 6
- inv_leaf: bfloat16 [16384, 128], P('cube'), as said below
- inv_lower: bfloat16 [16384, 128], P('cube'), as said below
- inv_upper: bfloat16 [16384, 128], P('cube'), as said below
- inv_root: bfloat16 [16384, 128], P('cube'), as said below
- pivots_leaf: int32 [8, 2], replicated, may hold values from 0 to 15, as said below
- pivots_lower: int32 [4, 2], replicated, may hold values from 0 to 31, as said below
- pivots_upper: int32 [2, 2], replicated, may hold values from 0 to 63, as said below
- pivots_root: int32 [1, 2], replicated, may hold values from 0 to 127, as said below
- child_sides: int32 [3, 128], replicated, may hold values from 0 to 1
Outputs:
- factored_leaf: float32 [2048, 16384], P(None, 'cube')
- factored_lower: float32 [4096, 16384], P(None, 'cube')
- factored_upper: float32 [8192, 16384], P(None, 'cube')
- factored_root: float32 [16384, 16384], P(None, 'cube')
The draws below stay inside these ranges and needn't reach their ends.
Inputs may be any that keep to these rules, and one draw needn't show every extreme that they name: `pivots_leaf`: each row holds 2 different block positions of its front. `pivots_lower`: each row holds 2 different block positions of its front. `pivots_upper`: each row holds 2 different block positions of its front. `pivots_root`: the row holds 2 different block positions of the root front. `inv_leaf`: each 128 x 128 block has positive diagonal entries from 1/64 to 1/16 and small entries of either sign elsewhere. `inv_lower`: as for inv_leaf. `inv_upper`: as for inv_leaf. `inv_root`: as for inv_leaf.
All inputs are finite; a program needn't handle non-finite values.
Results may differ from the reference program's by a relative error of at most 0.025.
Values may be sent and summed in bfloat16 or wider, within the bound.
No kernel may reach another device: no remote copies, remote signals or barrier semaphores. Data moves between devices by JAX's collectives and lax.ppermute only.
A program may use at most 128 MiB of HBM per device.

```python
import math
import jax
import jax.numpy as jnp
from jax import lax

BLOCK = 128
PIVOTS = 2
W0 = 2048
W1 = 4096
W2 = 8192
W3 = 16384
COLS = 16384
N_CUBE = 128


def inverse_blocks(diag_key, noise):
    row_ids = lax.broadcasted_iota(jnp.int32, (COLS, BLOCK), 0)
    col_ids = lax.broadcasted_iota(jnp.int32, (COLS, BLOCK), 1)
    diagonal = jnp.exp(jax.random.uniform(diag_key, (COLS, BLOCK), jnp.float32, math.log(1.0 / 64.0), math.log(1.0 / 16.0)))
    return jnp.where(row_ids % BLOCK == col_ids, diagonal, noise * (0.5 / BLOCK)).astype(jnp.bfloat16)


def choose_pivots(key, front_count, groups):
    front_keys = jax.random.split(key, front_count)
    chosen = jax.vmap(lambda subkey: jax.random.permutation(subkey, groups)[:PIVOTS])(front_keys).astype(jnp.int32)
    first_row = chosen[0]
    has_last = jnp.any(first_row == groups - 1)
    forced = first_row.at[1].set(groups - 1)
    first_row = jnp.where(has_last, first_row, forced).astype(jnp.int32)
    return chosen.at[0].set(first_row).astype(jnp.int32)


def draw_inv_leaf(key, part):
    key = jax.random.fold_in(key, 11)
    noise_key, diag_key = jax.random.split(key)
    noise = jnp.clip(jax.random.normal(noise_key, (COLS, BLOCK), jnp.float32), -4.0, 4.0)
    return inverse_blocks(diag_key, noise)


def draw_inv_lower(key, part):
    key = jax.random.fold_in(key, 12)
    noise_key, diag_key = jax.random.split(key)
    noise = jnp.clip(jax.random.normal(noise_key, (COLS, BLOCK), jnp.float32), -4.0, 4.0)
    return inverse_blocks(diag_key, noise)


def draw_inv_upper(key, part):
    key = jax.random.fold_in(key, 13)
    noise_key, diag_key = jax.random.split(key)
    noise = jnp.clip(jax.random.normal(noise_key, (COLS, BLOCK), jnp.float32), -4.0, 4.0)
    return inverse_blocks(diag_key, noise)


def draw_inv_root(key, part):
    key = jax.random.fold_in(key, 14)
    noise_key, diag_key = jax.random.split(key)
    noise = jnp.clip(jax.random.normal(noise_key, (COLS, BLOCK), jnp.float32), -4.0, 4.0)
    return inverse_blocks(diag_key, noise)


def draw_pivots_leaf(key, part):
    key = jax.random.fold_in(key, 21)
    return choose_pivots(key, 8, W0 // BLOCK)


def draw_pivots_lower(key, part):
    key = jax.random.fold_in(key, 22)
    return choose_pivots(key, 4, W1 // BLOCK)


def draw_pivots_upper(key, part):
    key = jax.random.fold_in(key, 23)
    return choose_pivots(key, 2, W2 // BLOCK)


def draw_pivots_root(key, part):
    key = jax.random.fold_in(key, 24)
    return choose_pivots(key, 1, W3 // BLOCK)


def touch_ends(drawn, key, smallest, largest):
    shape = drawn.shape
    spot = [jax.random.randint(jax.random.fold_in(key, axis), (), 0, shape[axis]) for axis in range(len(shape))]
    drawn = drawn.at[tuple(spot)].set(smallest)
    longest = shape.index(max(shape))
    spot[longest] = (spot[longest] + 1) % shape[longest]
    return drawn.at[tuple(spot)].set(largest)


def block_scale(stream_key, shape, shards, low, high):
    def one(position, shards_of):
        heights = jax.random.uniform(jax.random.fold_in(jax.random.fold_in(stream_key, 6), position), (shards_of,), jnp.float32, low / len(shards), high / len(shards))
        return jnp.repeat(jnp.exp(heights), shape[position] // shards_of).reshape((-1,) + (1,) * (len(shape) - position - 1))

    loudness = one(*shards[0])
    for cut in shards[1:]:
        loudness = loudness * one(*cut)
    return loudness


def normal_values(rng, dims, deviation, most, shards=(), kind=jnp.bfloat16):
    drawn = deviation * jax.random.normal(rng, dims, jnp.float32)
    if shards:
        drawn = drawn * block_scale(rng, dims, shards, -0.22, 0.18)
    return jnp.clip(drawn, -most, most).astype(kind)


def setup_inputs(seed: int = 0) -> dict:
    arg_keys = jax.random.split(jax.random.key(seed), 14)
    front_leaf = normal_values(arg_keys[0], (W0, COLS), 1.0, 6.0, ((1, 128),))
    front_lower = normal_values(arg_keys[1], (W1, COLS), 1.0, 6.0, ((1, 128),))
    front_upper = normal_values(arg_keys[2], (W2, COLS), 1.0, 6.0, ((1, 128),))
    front_root = normal_values(arg_keys[3], (W3, COLS), 1.0, 6.0, ((1, 128),))
    inv_leaf = draw_inv_leaf(jax.random.fold_in(arg_keys[13], 71), 0)
    inv_lower = draw_inv_lower(jax.random.fold_in(arg_keys[13], 71), 0)
    inv_upper = draw_inv_upper(jax.random.fold_in(arg_keys[13], 71), 0)
    inv_root = draw_inv_root(jax.random.fold_in(arg_keys[13], 71), 0)
    pivots_leaf = draw_pivots_leaf(jax.random.fold_in(arg_keys[13], 71), 0)
    pivots_lower = draw_pivots_lower(jax.random.fold_in(arg_keys[13], 71), 0)
    pivots_upper = draw_pivots_upper(jax.random.fold_in(arg_keys[13], 71), 0)
    pivots_root = draw_pivots_root(jax.random.fold_in(arg_keys[13], 71), 0)
    child_sides = touch_ends(jax.random.randint(arg_keys[12], (3, N_CUBE), 0, 2), jax.random.fold_in(arg_keys[12], 1), 0, 1).astype(jnp.int32)
    return dict(front_leaf=front_leaf, front_lower=front_lower, front_upper=front_upper, front_root=front_root, inv_leaf=inv_leaf, inv_lower=inv_lower, inv_upper=inv_upper, inv_root=inv_root, pivots_leaf=pivots_leaf, pivots_lower=pivots_lower, pivots_upper=pivots_upper, pivots_root=pivots_root, child_sides=child_sides)


def eliminate(matrix, pivot_row, inverse_rows, front_num, block_cols):
    front_width = matrix.shape[0]
    groups = front_width // block_cols
    block_ids = jnp.arange(front_width, dtype=jnp.int32) // block_cols
    done_rows = jnp.zeros((front_width,), jnp.bool_)
    for panel_num in range(PIVOTS):
        pivot_blk = pivot_row[panel_num].astype(jnp.int32)
        panel = lax.dynamic_slice_in_dim(matrix, pivot_blk * block_cols, block_cols, 1)
        inverse = lax.dynamic_slice_in_dim(inverse_rows, (front_num * groups + pivot_blk) * block_cols, block_cols, 0)
        rounded = jnp.dot(panel, inverse, precision=lax.Precision.HIGHEST).astype(jnp.bfloat16)
        factor = lax.optimization_barrier(rounded).astype(matrix.dtype)
        done_rows = done_rows | (block_ids == pivot_blk)
        pivot_band = lax.dynamic_slice_in_dim(matrix, pivot_blk * block_cols, block_cols, 0)
        masked = jnp.where(done_rows[:, None], jnp.zeros_like(factor), factor)
        update = jnp.dot(masked, pivot_band, precision=lax.Precision.HIGHEST)
        matrix = jnp.where(done_rows[None, :], matrix, matrix - update)
        matrix = lax.dynamic_update_slice_in_dim(matrix, factor, pivot_blk * block_cols, 1)
    return matrix


def add_child(carried, matrix, pivot_row, side_row, block_cols):
    front_width = matrix.shape[0]
    groups = front_width // block_cols
    blocks = jnp.arange(groups, dtype=jnp.int32)
    keep_blocks = jnp.logical_not(jnp.any(blocks[:, None] == pivot_row[None, :].astype(jnp.int32), axis=1))
    positions = (blocks + groups * side_row.astype(jnp.int32)).astype(jnp.int32)
    blocked = matrix.reshape(groups, block_cols, groups, block_cols)
    keep_both = keep_blocks[:, None, None, None] & keep_blocks[None, None, :, None]
    kept = jnp.where(keep_both, blocked, jnp.zeros_like(blocked))
    lifted = jnp.zeros((2 * groups, block_cols, groups, block_cols), matrix.dtype).at[positions].add(kept)
    widened = carried.reshape(2 * groups, block_cols, 2 * groups, block_cols).at[:, :, positions].add(lifted)
    return widened.reshape(2 * front_width, 2 * front_width)


def reference(front_leaf, front_lower, front_upper, front_root, inv_leaf, inv_lower, inv_upper, inv_root, pivots_leaf, pivots_lower, pivots_upper, pivots_root, child_sides):
    fronts = (front_leaf, front_lower, front_upper, front_root)
    inverses = (inv_leaf, inv_lower, inv_upper, inv_root)
    tables = (pivots_leaf, pivots_lower, pivots_upper, pivots_root)
    block_cols = BLOCK
    outputs = []
    carried_list = []
    for tier_num in range(4):
        front_width = fronts[tier_num].shape[0]
        groups = front_width // block_cols
        front_count = fronts[tier_num].shape[1] // front_width
        finished = []
        for front_num in range(front_count):
            matrix = fronts[tier_num][:, front_num * front_width:(front_num + 1) * front_width].astype(jnp.float32)
            if tier_num > 0:
                summed = (matrix + carried_list[front_num]).astype(jnp.bfloat16)
                matrix = lax.optimization_barrier(summed).astype(jnp.float32)
            finished.append(eliminate(matrix, tables[tier_num][front_num], inverses[tier_num].astype(jnp.float32), front_num, block_cols))
        outputs.append(jnp.concatenate(finished, axis=1))
        if tier_num < 3:
            carried_list = []
            for parent_num in range(front_count // 2):
                carried = jnp.zeros((2 * front_width, 2 * front_width), jnp.float32)
                for child_num in (2 * parent_num, 2 * parent_num + 1):
                    side_row = child_sides[tier_num, child_num * groups:(child_num + 1) * groups]
                    carried = add_child(carried, finished[child_num], tables[tier_num][child_num], side_row, block_cols)
                carried_list.append(carried)
    return outputs[0], outputs[1], outputs[2], outputs[3]
```

```python
import jax
import jax.numpy as jnp
from jax import lax
from jax.sharding import PartitionSpec as P

AXIS = "cube"
SHIFT = {"y": 5, "z": 3, "x": 1}


def permute(array, pairs):
    return lax.ppermute(array, AXIS, pairs)


def moved(device, axis, count, step):
    shift = SHIFT[axis]
    position = (device >> shift) & (count - 1)
    return device - (position << shift) + (((position + step) % count) << shift)


STAGES = (
    ((("z", "z"), 2), (("x", "x"), 4)),
    ((("x", "z"), 4), (("z", "x"), 4)),
    ((("y", "y"), 2), (("x", "z"), 4), (("z", "x"), 4)),
    ((("x", "y"), 4), (("z", "x"), 4), (("y", "z"), 4)),
)


def gather_stage(block, device, axes, count):
    devices = lax.axis_size(AXIS)
    pieces = [block]
    for step in range(1, count):
        pairs = [(moved(i, axes[i & 1], count, step), i) for i in range(devices)]
        pieces.append(permute(block, pairs))
    position = jnp.where(
        device & 1 == 0,
        (device >> SHIFT[axes[0]]) & (count - 1),
        (device >> SHIFT[axes[1]]) & (count - 1),
    )
    placed = []
    for spot in range(count):
        which = jnp.bitwise_and(spot - position, count - 1)
        if count == 2:
            placed.append(jnp.where(which == 0, pieces[0], pieces[1]))
        else:
            placed.append(lax.select_n(which, *pieces))
    return jnp.stack(placed, 0)


def gather_rows(block, device, tier_num):
    rows, cols = block.shape
    devices = lax.axis_size(AXIS)
    stages = STAGES[tier_num]
    half = block
    for axes, count in stages:
        half = gather_stage(half, device, axes, count)
    other = permute(half, [(i, i ^ 1) for i in range(devices)])
    even = jnp.where(device & 1 == 0, half, other)
    odd = jnp.where(device & 1 == 0, other, half)
    order = sorted(a for (a, _), _ in stages)
    order = [a for a in "yzx" if a in order]
    halves = []
    for core, part in ((0, even), (1, odd)):
        held = [axes[core] for axes, _ in reversed(stages)]
        turn = [held.index(a) for a in order]
        part = jnp.transpose(part, turn + [len(turn), len(turn) + 1])
        halves.append(part.reshape(-1, rows, cols))
    return jnp.stack(halves, 1).reshape(-1, rows, cols)


def shards(
    front_leaf,
    front_lower,
    front_upper,
    front_root,
    inv_leaf,
    inv_lower,
    inv_upper,
    inv_root,
    pivots_leaf,
    pivots_lower,
    pivots_upper,
    pivots_root,
    child_sides,
):
    fronts = (front_leaf, front_lower, front_upper, front_root)
    inverses = (inv_leaf, inv_lower, inv_upper, inv_root)
    tables = (pivots_leaf, pivots_lower, pivots_upper, pivots_root)
    device = lax.axis_index(AXIS)
    devices = lax.axis_size(AXIS)
    width = front_leaf.shape[1]
    column = front_leaf
    results = []
    for tier_num in range(4):
        groups = fronts[tier_num].shape[0] // width
        front_num = device // groups
        local = device % groups
        teams = [list(range(i, i + groups)) for i in range(0, devices, groups)]
        table = tables[tier_num]
        pivot_row = lax.dynamic_index_in_dim(table, front_num, 0, keepdims=False)
        first, second = pivot_row[0], pivot_row[1]
        is_first, is_second = local == first, local == second

        scaled = jnp.dot(column, inverses[tier_num], preferred_element_type=jnp.float32)
        scaled = scaled.astype(jnp.bfloat16)
        rows = lax.all_to_all(
            scaled.reshape(groups, width, width), AXIS, 0, 0, axis_index_groups=teams, tiled=True
        )
        own = jnp.concatenate(
            [
                lax.dynamic_index_in_dim(rows, first, 0, keepdims=False),
                lax.dynamic_index_in_dim(rows, second, 0, keepdims=False),
            ],
            1,
        )
        panels = gather_rows(own, device, tier_num)
        blocks = jnp.arange(groups, dtype=jnp.int32)
        live_first = (blocks != first)[:, None, None]
        live = ((blocks != first) & (blocks != second))[:, None, None]
        zero = jnp.zeros((), jnp.bfloat16)
        factor0 = panels[:, :, :width]
        scaled1 = panels[:, :, width:]
        masked0 = jnp.where(live_first, factor0, zero).reshape(-1, width)
        top1 = lax.dynamic_index_in_dim(scaled1, first, 0, keepdims=False)
        change1 = jnp.dot(masked0, top1, preferred_element_type=jnp.float32)
        factor1 = (scaled1.reshape(-1, width).astype(jnp.float32) - change1).astype(jnp.bfloat16)
        masked1 = jnp.where(live, factor1.reshape(groups, width, width), zero).reshape(-1, width)

        cube = column.reshape(groups, width, width)
        band0 = lax.dynamic_index_in_dim(cube, first, 0, keepdims=False)
        band1 = lax.dynamic_index_in_dim(cube, second, 0, keepdims=False)
        fac01 = lax.dynamic_index_in_dim(factor0, second, 0, keepdims=False)
        band1 = (
            band1.astype(jnp.float32) - jnp.dot(fac01, band0, preferred_element_type=jnp.float32)
        ).astype(jnp.bfloat16)
        update = jnp.dot(
            jnp.concatenate([masked0, masked1], 1),
            jnp.concatenate([band0, band1], 0),
            preferred_element_type=jnp.float32,
        )
        final = jnp.where(
            is_first,
            factor0.reshape(-1, width).astype(jnp.float32),
            jnp.where(
                is_second, factor1.astype(jnp.float32), column.astype(jnp.float32) - update
            ),
        )
        results.append(final)
        if tier_num < 3:
            sent = final.astype(jnp.bfloat16)
            received = permute(sent, [(i, i ^ groups) for i in range(devices)])
            side_row = child_sides[tier_num]
            parent_half = (device // groups) & 1
            total = fronts[tier_num + 1].reshape(2, groups, width, width).astype(jnp.float32)
            halves = jnp.arange(2, dtype=jnp.int32)
            for part, flip in ((final.reshape(groups, width, width), 0), (received.reshape(groups, width, width), 1)):
                front_of = front_num ^ flip
                pivots_of = lax.dynamic_index_in_dim(table, front_of, 0, keepdims=False)
                sides = lax.dynamic_slice_in_dim(side_row, front_of * groups, groups, 0)
                stays = (blocks != pivots_of[0]) & (blocks != pivots_of[1])
                lands = (
                    (lax.dynamic_index_in_dim(side_row, front_of * groups + local, 0, keepdims=False) == parent_half)
                    & (local != pivots_of[0])
                    & (local != pivots_of[1])
                )
                keep = (sides[None, :] == halves[:, None]) & stays[None, :] & lands
                total = total + jnp.where(
                    keep[:, :, None, None], part[None].astype(jnp.float32), 0.0
                )
            column = total.astype(jnp.bfloat16).reshape(-1, width)
    return tuple(results)


def solution(mesh):
    across, down, whole = P(None, AXIS), P(AXIS, None), P()
    return jax.shard_map(
        shards,
        mesh=mesh,
        in_specs=(across,) * 4 + (down,) * 4 + (whole,) * 5,
        out_specs=(across,) * 4,
        check_vma=False,
    )
```

```python
import functools

import jax
import jax.numpy as jnp
from jax import lax
from jax.experimental import pallas as pl
from jax.experimental.pallas import tpu as pltpu
from jax.sharding import PartitionSpec as P

AXIS = "cube"
SHIFT = {"y": 5, "z": 3, "x": 1}


def permute(array, pairs):
    return lax.ppermute(array, AXIS, pairs)


def moved(device, axis, count, step):
    shift = SHIFT[axis]
    position = (device >> shift) & (count - 1)
    return device - (position << shift) + (((position + step) % count) << shift)


STAGES = (
    ((("z", "z"), 2), (("x", "x"), 4)),
    ((("x", "z"), 4), (("z", "x"), 4)),
    ((("y", "y"), 2), (("x", "z"), 4), (("z", "x"), 4)),
    ((("x", "y"), 4), (("z", "x"), 4), (("y", "z"), 4)),
)


def axis_position(device, axis, count):
    return (device >> SHIFT[axis]) & (count - 1)


def gather_pieces(block, axes, count):
    devices = lax.axis_size(AXIS)
    pieces = [block]
    for step in range(1, count):
        pieces.append(permute(block, [(moved(i, axes[i & 1], count, step), i) for i in range(devices)]))
    return pieces


def gather_stage(block, device, axes, count):
    pieces = gather_pieces(block, axes, count)
    position = jnp.where(
        device & 1 == 0, axis_position(device, axes[0], count), axis_position(device, axes[1], count)
    )
    placed = []
    for spot in range(count):
        which = jnp.bitwise_and(spot - position, count - 1)
        if count == 2:
            placed.append(jnp.where(which == 0, pieces[0], pieces[1]))
        else:
            placed.append(lax.select_n(which, *pieces))
    return jnp.concatenate(placed, 0)


def gather_rows(block, device, tier_num):
    devices = lax.axis_size(AXIS)
    stages = STAGES[tier_num]
    half = block[None]
    for axes, count in stages[:-1]:
        half = gather_stage(half, device, axes, count)
    axes, count = stages[-1]
    pieces = gather_pieces(half, axes, count)
    others = [permute(piece, [(i, i ^ 1) for i in range(devices)]) for piece in pieces]
    return pieces, others


def place_of(tier_num, groups, r):
    places = []
    for core in range(2):
        place, scale = 0, 1
        for axes, count in STAGES[tier_num]:
            place = place + axis_position(r, axes[core], count) * scale
            scale *= count
        places.append(place + core * (groups // 2))
    return jnp.where(r & 1 == 0, places[0], places[1])


ROLE_NONE, ROLE_FIRST, ROLE_SECOND = 0, 1, 2


def tier_kernel(tier_num, groups, width, span, count, info, column_any, column_ref, *refs):
    pieces, (final_ref, kept_ref, panel, band, bands_in, sems, band_sems) = (
        refs[: 2 * count],
        refs[2 * count :],
    )
    first, second, role, core = info[0], info[1], info[2], info[3]
    place = functools.partial(place_of, tier_num, groups)
    chunk = pl.program_id(0)
    part = groups // (2 * count)
    zero = jnp.zeros((width, width), jnp.bfloat16)

    @pl.when(chunk == 0)
    def _():
        copies = []
        for side in range(2):
            holder = core if side == 0 else 1 - core
            position = jnp.where(holder == 0, info[4], info[5])
            for step in range(count):
                slot = holder * (groups // 2) + ((position + step) & (count - 1)) * part
                copies.append(
                    pltpu.make_async_copy(
                        pieces[side * count + step],
                        panel.at[pl.ds(slot, part)],
                        sems.at[side * count + step],
                    )
                )
        for which, block in ((0, first), (1, second)):
            copies.append(
                pltpu.make_async_copy(
                    column_any.at[pl.ds(pl.multiple_of(block * width, width), width)],
                    bands_in.at[which],
                    band_sems.at[which],
                )
            )
        for copy in copies:
            copy.start()
        for copy in copies:
            copy.wait()
        at_first, at_second = place(first), place(second)
        top = panel[at_first, :, width:]

        def scale_rows(i, carry):
            both = panel[pl.ds(i * span, span)].reshape(span * width, 2 * width)
            change = jnp.dot(both[:, :width], top, preferred_element_type=jnp.float32)
            fixed = (both[:, width:].astype(jnp.float32) - change).astype(jnp.bfloat16)
            panel[pl.ds(i * span, span), :, width:] = fixed.reshape(span, width, width)
            return carry

        lax.fori_loop(0, groups // span, scale_rows, 0)
        panel[at_first, :, width:] = top
        lower = bands_in[1].astype(jnp.float32) - jnp.dot(
            panel[at_second, :, :width], bands_in[0], preferred_element_type=jnp.float32
        )
        band[:width] = bands_in[0]
        band[width:] = lower.astype(jnp.bfloat16)

        @pl.when(role == ROLE_NONE)
        def _():
            panel[at_first, :, :width] = zero
            panel[at_first, :, width:] = zero
            panel[at_second, :, width:] = zero

    for j in range(span):
        r = chunk * span + j
        rows = pl.ds(j * width, width)
        at = place(r)

        @pl.when(role == ROLE_NONE)
        def _():
            update = jnp.dot(panel[at], band[...], preferred_element_type=jnp.float32)
            value = column_ref[rows].astype(jnp.float32) - update
            final_ref[rows] = value
            if kept_ref is not None:
                value = jnp.where((r == first) | (r == second), 0.0, value)
                kept_ref[rows] = value.astype(jnp.bfloat16)

        @pl.when(role == ROLE_FIRST)
        def _():
            final_ref[rows] = panel[at, :, :width].astype(jnp.float32)

        @pl.when(role == ROLE_SECOND)
        def _():
            final_ref[rows] = panel[at, :, width:].astype(jnp.float32)

        if kept_ref is not None:

            @pl.when(role != ROLE_NONE)
            def _():
                kept_ref[rows] = zero


def eliminate(tier_num, column, pieces, others, info, keep):
    rows, width = column.shape
    groups = rows // width
    count = len(pieces)
    span = min(8, groups)
    block = pl.BlockSpec((span * width, width), lambda i, info: (i, 0))
    anywhere = pl.BlockSpec(memory_space=pl.ANY)
    body = functools.partial(tier_kernel, tier_num, groups, width, span, count)
    if not keep:
        inner = body

        def body(info, column_any, column_ref, *refs):
            at = 2 * count + 1
            inner(info, column_any, column_ref, *refs[:at], None, *refs[at:])

    out_shape = [jax.ShapeDtypeStruct((rows, width), jnp.float32)]
    if keep:
        out_shape.append(jax.ShapeDtypeStruct((rows, width), jnp.bfloat16))
    return pl.pallas_call(
        body,
        grid_spec=pltpu.PrefetchScalarGridSpec(
            num_scalar_prefetch=1,
            grid=(groups // span,),
            in_specs=[anywhere, block] + [anywhere] * (2 * count),
            out_specs=[block] * len(out_shape),
            scratch_shapes=[
                pltpu.VMEM((groups, width, 2 * width), jnp.bfloat16),
                pltpu.VMEM((2 * width, width), jnp.bfloat16),
                pltpu.VMEM((2, width, width), jnp.bfloat16),
                pltpu.SemaphoreType.DMA((2 * count,)),
                pltpu.SemaphoreType.DMA((2,)),
            ],
        ),
        out_shape=out_shape,
        compiler_params=pltpu.CompilerParams(vmem_limit_bytes=32 * 1024 * 1024),
        cost_estimate=pl.CostEstimate(
            flops=6 * rows * width * width, bytes_accessed=12 * rows * width, transcendentals=0
        ),
    )(info, column, column, *pieces, *others)


def shards(
    front_leaf,
    front_lower,
    front_upper,
    front_root,
    inv_leaf,
    inv_lower,
    inv_upper,
    inv_root,
    pivots_leaf,
    pivots_lower,
    pivots_upper,
    pivots_root,
    child_sides,
):
    fronts = (front_leaf, front_lower, front_upper, front_root)
    inverses = (inv_leaf, inv_lower, inv_upper, inv_root)
    tables = (pivots_leaf, pivots_lower, pivots_upper, pivots_root)
    device = lax.axis_index(AXIS)
    devices = lax.axis_size(AXIS)
    width = front_leaf.shape[1]
    column = front_leaf
    results = []
    for tier_num in range(4):
        groups = fronts[tier_num].shape[0] // width
        front_num = device // groups
        local = device % groups
        teams = [list(range(i, i + groups)) for i in range(0, devices, groups)]
        table = tables[tier_num]
        pivot_row = lax.dynamic_index_in_dim(table, front_num, 0, keepdims=False)
        first, second = pivot_row[0], pivot_row[1]
        is_first, is_second = local == first, local == second

        scaled = jnp.dot(column, inverses[tier_num], preferred_element_type=jnp.float32)
        scaled = scaled.astype(jnp.bfloat16)
        rows = lax.all_to_all(
            scaled.reshape(groups, width, width), AXIS, 0, 0, axis_index_groups=teams, tiled=True
        )
        own = jnp.concatenate(
            [
                lax.dynamic_index_in_dim(rows, first, 0, keepdims=False),
                lax.dynamic_index_in_dim(rows, second, 0, keepdims=False),
            ],
            1,
        )
        pieces, others = gather_rows(own, device, tier_num)
        axes, count = STAGES[tier_num][-1]
        role = jnp.where(is_first, ROLE_FIRST, jnp.where(is_second, ROLE_SECOND, ROLE_NONE))
        info = jnp.stack(
            [
                first,
                second,
                role,
                device & 1,
                axis_position(device, axes[0], count),
                axis_position(device, axes[1], count),
            ]
        ).astype(jnp.int32)
        made = eliminate(tier_num, column, pieces, others, info, tier_num < 3)
        results.append(made[0])
        if tier_num < 3:
            kept = made[1]
            received = permute(kept, [(i, i ^ groups) for i in range(devices)])
            blocks = jnp.arange(groups, dtype=jnp.int32)
            side_row = child_sides[tier_num]
            parent_half = (device // groups) & 1
            total = fronts[tier_num + 1].reshape(2, groups, width, width).astype(jnp.float32)
            halves = jnp.arange(2, dtype=jnp.int32)
            for part, flip in ((kept.reshape(groups, width, width), 0), (received.reshape(groups, width, width), 1)):
                front_of = front_num ^ flip
                sides = lax.dynamic_slice_in_dim(side_row, front_of * groups, groups, 0)
                own_side = lax.dynamic_index_in_dim(
                    side_row, front_of * groups + local, 0, keepdims=False
                )
                keep = (sides[None, :] == halves[:, None]) & (own_side == parent_half)
                total = total + jnp.where(
                    keep[:, :, None, None], part[None].astype(jnp.float32), 0.0
                )
            column = total.astype(jnp.bfloat16).reshape(-1, width)
    return tuple(results)


def solution(mesh):
    across, down, whole = P(None, AXIS), P(AXIS, None), P()
    return jax.shard_map(
        shards,
        mesh=mesh,
        in_specs=(across,) * 4 + (down,) * 4 + (whole,) * 5,
        out_specs=(across,) * 4,
        check_vma=False,
    )
```

```python
import functools

import jax
import jax.numpy as jnp
from jax import lax
from jax.experimental import pallas as pl
from jax.experimental.pallas import tpu as pltpu
from jax.sharding import PartitionSpec as P

AXIS = "cube"
SHIFT = {"y": 5, "z": 3, "x": 1}


def permute(array, pairs):
    return lax.ppermute(array, AXIS, pairs)


def moved(device, axis, count, step):
    shift = SHIFT[axis]
    position = (device >> shift) & (count - 1)
    return device - (position << shift) + (((position + step) % count) << shift)


STAGES = (
    ((("z", "z"), 2), (("x", "x"), 4)),
    ((("x", "z"), 4), (("z", "x"), 4)),
    ((("y", "y"), 2), (("x", "z"), 4), (("z", "x"), 4)),
    ((("y", "y"), 4), (("x", "z"), 4), (("z", "x"), 4)),
)


def axis_position(device, axis, count):
    return (device >> SHIFT[axis]) & (count - 1)


def gather_pieces(block, axes, count):
    devices = lax.axis_size(AXIS)
    pieces = [block]
    for step in range(1, count):
        pieces.append(permute(block, [(moved(i, axes[i & 1], count, step), i) for i in range(devices)]))
    return pieces


def gather_stage(block, device, axes, count):
    pieces = gather_pieces(block, axes, count)
    position = jnp.where(
        device & 1 == 0, axis_position(device, axes[0], count), axis_position(device, axes[1], count)
    )
    placed = []
    for spot in range(count):
        which = jnp.bitwise_and(spot - position, count - 1)
        if count == 2:
            placed.append(jnp.where(which == 0, pieces[0], pieces[1]))
        else:
            placed.append(lax.select_n(which, *pieces))
    return jnp.concatenate(placed, 0)


def gather_rows(block, device, tier_num, early):
    devices = lax.axis_size(AXIS)
    stages = STAGES[tier_num]
    half = block[None]
    for axes, count in stages[:-1]:
        half = gather_stage(half, device, axes, count)
    if early is not None:
        half, early = lax.optimization_barrier((half, early))
    axes, count = stages[-1]
    pieces = gather_pieces(half, axes, count)
    others = [permute(piece, [(i, i ^ 1) for i in range(devices)]) for piece in pieces]
    return pieces, others, early


def place_of(tier_num, groups, r):
    places = []
    for core in range(2):
        place, scale = 0, 1
        for axes, count in STAGES[tier_num]:
            place = place + axis_position(r, axes[core], count) * scale
            scale *= count
        places.append(place + core * (groups // 2))
    return jnp.where(r & 1 == 0, places[0], places[1])


ROLE_NONE, ROLE_FIRST, ROLE_SECOND = 0, 1, 2


def tier_kernel(tier_num, groups, width, span, count, info, column_any, column_ref, *refs):
    pieces, (final_ref, kept_ref, panel, band, bands_in, sems, band_sems) = (
        refs[: 2 * count],
        refs[2 * count :],
    )
    first, second, role, core = info[0], info[1], info[2], info[3]
    place = functools.partial(place_of, tier_num, groups)
    chunk = pl.program_id(0)
    part = groups // (2 * count)
    zero = jnp.zeros((width, width), jnp.bfloat16)

    @pl.when(chunk == 0)
    def _():
        copies = []
        for side in range(2):
            holder = core if side == 0 else 1 - core
            position = jnp.where(holder == 0, info[4], info[5])
            for step in range(count):
                slot = holder * (groups // 2) + ((position + step) & (count - 1)) * part
                copies.append(
                    pltpu.make_async_copy(
                        pieces[side * count + step],
                        panel.at[pl.ds(slot, part)],
                        sems.at[side * count + step],
                    )
                )
        for which, block in ((0, first), (1, second)):
            copies.append(
                pltpu.make_async_copy(
                    column_any.at[pl.ds(pl.multiple_of(block * width, width), width)],
                    bands_in.at[which],
                    band_sems.at[which],
                )
            )
        for copy in copies:
            copy.start()
        for copy in copies:
            copy.wait()
        at_first, at_second = place(first), place(second)
        top = panel[at_first, :, width:]

        def scale_rows(i, carry):
            both = panel[pl.ds(i * span, span)].reshape(span * width, 2 * width)
            change = jnp.dot(both[:, :width], top, preferred_element_type=jnp.float32)
            fixed = (both[:, width:].astype(jnp.float32) - change).astype(jnp.bfloat16)
            panel[pl.ds(i * span, span), :, width:] = fixed.reshape(span, width, width)
            return carry

        lax.fori_loop(0, groups // span, scale_rows, 0)
        panel[at_first, :, width:] = top
        lower = bands_in[1].astype(jnp.float32) - jnp.dot(
            panel[at_second, :, :width], bands_in[0], preferred_element_type=jnp.float32
        )
        band[:width] = bands_in[0]
        band[width:] = lower.astype(jnp.bfloat16)

        @pl.when(role == ROLE_NONE)
        def _():
            panel[at_first, :, :width] = zero
            panel[at_first, :, width:] = zero
            panel[at_second, :, width:] = zero

    places = [place(chunk * span + j) for j in range(span)]

    @pl.when(role == ROLE_NONE)
    def _():
        both = jnp.concatenate([panel[at] for at in places], 0)
        update = jnp.dot(both, band[...], preferred_element_type=jnp.float32)
        value = column_ref[...].astype(jnp.float32) - update
        final_ref[...] = value
        if kept_ref is not None:
            kept_ref[...] = value.astype(jnp.bfloat16)
            for block in (first, second):

                @pl.when((block >= chunk * span) & (block < (chunk + 1) * span))
                def _():
                    spot = pl.multiple_of((block - chunk * span) * width, width)
                    kept_ref[pl.ds(spot, width)] = zero

    for j in range(span):
        rows = pl.ds(j * width, width)
        at = places[j]

        @pl.when(role == ROLE_FIRST)
        def _():
            final_ref[rows] = panel[at, :, :width].astype(jnp.float32)

        @pl.when(role == ROLE_SECOND)
        def _():
            final_ref[rows] = panel[at, :, width:].astype(jnp.float32)

    if kept_ref is not None:

        @pl.when(role != ROLE_NONE)
        def _():
            kept_ref[...] = jnp.zeros_like(kept_ref)


def eliminate(tier_num, column, pieces, others, info, keep):
    rows, width = column.shape
    groups = rows // width
    count = len(pieces)
    span = min(8, groups)
    block = pl.BlockSpec((span * width, width), lambda i, info: (i, 0))
    anywhere = pl.BlockSpec(memory_space=pl.ANY)
    body = functools.partial(tier_kernel, tier_num, groups, width, span, count)
    if not keep:
        inner = body

        def body(info, column_any, column_ref, *refs):
            at = 2 * count + 1
            inner(info, column_any, column_ref, *refs[:at], None, *refs[at:])

    out_shape = [jax.ShapeDtypeStruct((rows, width), jnp.float32)]
    if keep:
        out_shape.append(jax.ShapeDtypeStruct((rows, width), jnp.bfloat16))
    return pl.pallas_call(
        body,
        grid_spec=pltpu.PrefetchScalarGridSpec(
            num_scalar_prefetch=1,
            grid=(groups // span,),
            in_specs=[anywhere, block] + [anywhere] * (2 * count),
            out_specs=[block] * len(out_shape),
            scratch_shapes=[
                pltpu.VMEM((groups, width, 2 * width), jnp.bfloat16),
                pltpu.VMEM((2 * width, width), jnp.bfloat16),
                pltpu.VMEM((2, width, width), jnp.bfloat16),
                pltpu.SemaphoreType.DMA((2 * count,)),
                pltpu.SemaphoreType.DMA((2,)),
            ],
        ),
        out_shape=out_shape,
        compiler_params=pltpu.CompilerParams(vmem_limit_bytes=32 * 1024 * 1024),
        cost_estimate=pl.CostEstimate(
            flops=6 * rows * width * width, bytes_accessed=12 * rows * width, transcendentals=0
        ),
    )(info, column, column, *pieces, *others)


def shards(
    front_leaf,
    front_lower,
    front_upper,
    front_root,
    inv_leaf,
    inv_lower,
    inv_upper,
    inv_root,
    pivots_leaf,
    pivots_lower,
    pivots_upper,
    pivots_root,
    child_sides,
):
    fronts = (front_leaf, front_lower, front_upper, front_root)
    inverses = (inv_leaf, inv_lower, inv_upper, inv_root)
    tables = (pivots_leaf, pivots_lower, pivots_upper, pivots_root)
    device = lax.axis_index(AXIS)
    devices = lax.axis_size(AXIS)
    width = front_leaf.shape[1]
    column = front_leaf
    results = []
    zero = jnp.zeros((), jnp.bfloat16)

    def pivots_of(tier_num):
        groups = fronts[tier_num].shape[0] // width
        row = lax.dynamic_index_in_dim(tables[tier_num], device // groups, 0, keepdims=False)
        return row[0], row[1]

    def pivot_pair(block, tier_num):
        first, second = pivots_of(tier_num)
        local = device % (fronts[tier_num].shape[0] // width)
        return jnp.concatenate(
            [jnp.where(local == first, block, zero), jnp.where(local == second, block, zero)], 1
        )

    bits = devices.bit_length() - 1
    scales = jnp.stack([pivot_pair(inv_upper, 2), pivot_pair(inv_root, 3)])
    for bit in range(bits - 1):
        scales = scales + permute(scales, [(i, i ^ (1 << bit)) for i in range(devices)])
    root_scale = scales[1] + permute(scales[1], [(i, i ^ (1 << (bits - 1))) for i in range(devices)])
    row_scales = {2: scales[0], 3: root_scale}

    def raw_rows(front, tier_num):
        groups = front.shape[0] // width
        teams = [list(range(i, i + groups)) for i in range(0, devices, groups)]
        rows = lax.all_to_all(
            front.reshape(groups, width, width), AXIS, 0, 0, axis_index_groups=teams, tiled=True
        )
        return jnp.concatenate(
            [lax.dynamic_index_in_dim(rows, block, 0, keepdims=False) for block in pivots_of(tier_num)],
            1,
        )

    upper_own = raw_rows(front_upper, 2)
    root_own = raw_rows(front_root, 3)
    carried_rows = None
    for tier_num in range(4):
        groups = fronts[tier_num].shape[0] // width
        front_num = device // groups
        local = device % groups
        teams = [list(range(i, i + groups)) for i in range(0, devices, groups)]
        table = tables[tier_num]
        pivot_row = lax.dynamic_index_in_dim(table, front_num, 0, keepdims=False)
        first, second = pivot_row[0], pivot_row[1]
        is_first, is_second = local == first, local == second

        if tier_num < 2:
            scaled = jnp.dot(column, inverses[tier_num], preferred_element_type=jnp.float32)
            scaled = scaled.astype(jnp.bfloat16)
            if tier_num == 1:
                scaled, upper_own, row_scales = lax.optimization_barrier((scaled, upper_own, row_scales))
            rows = lax.all_to_all(
                scaled.reshape(groups, width, width), AXIS, 0, 0, axis_index_groups=teams, tiled=True
            )
            own = jnp.concatenate(
                [
                    lax.dynamic_index_in_dim(rows, first, 0, keepdims=False),
                    lax.dynamic_index_in_dim(rows, second, 0, keepdims=False),
                ],
                1,
            )
        else:
            raw, scale = (upper_own if tier_num == 2 else root_own), row_scales[tier_num]
            summed = (raw.astype(jnp.float32) + carried_rows).astype(jnp.bfloat16)
            own = jnp.concatenate(
                [
                    jnp.dot(
                        summed[:, i : i + width],
                        scale[:, i : i + width],
                        preferred_element_type=jnp.float32,
                    ).astype(jnp.bfloat16)
                    for i in (0, width)
                ],
                1,
            )
        if tier_num < 2:
            pieces, others, _ = gather_rows(own, device, tier_num, None)
        else:
            pieces, others, upper_half = gather_rows(own, device, tier_num, received[0])
            column = assemble([upper_half, received[1]])
        axes, count = STAGES[tier_num][-1]
        role = jnp.where(is_first, ROLE_FIRST, jnp.where(is_second, ROLE_SECOND, ROLE_NONE))
        info = jnp.stack(
            [
                first,
                second,
                role,
                device & 1,
                axis_position(device, axes[0], count),
                axis_position(device, axes[1], count),
            ]
        ).astype(jnp.int32)
        made = eliminate(tier_num, column, pieces, others, info, tier_num < 3)
        results.append(made[0])
        if tier_num < 3:
            kept = made[1]
            side_row = child_sides[tier_num]
            parent_half = (device // groups) & 1
            if tier_num >= 1:
                if tier_num == 2:
                    kept, root_own = lax.optimization_barrier((kept, root_own))
                rows = lax.all_to_all(
                    kept.reshape(groups, width, width), AXIS, 0, 0, axis_index_groups=teams, tiled=True
                )
                found = []
                for pivot in pivots_of(tier_num + 1):
                    source = pivot % groups
                    reaches = side_row[front_num * groups + source] == pivot // groups
                    block = lax.dynamic_index_in_dim(rows, source, 0, keepdims=False)
                    found.append(jnp.where(reaches, block, zero))
                found = jnp.concatenate(found, 1)
                met = permute(found, [(i, i ^ groups) for i in range(devices)])
                carried_rows = jnp.where(
                    side_row[device] == parent_half, found.astype(jnp.float32), 0.0
                ) + jnp.where(side_row[device ^ groups] == parent_half, met.astype(jnp.float32), 0.0)
            swap = [(i, i ^ groups) for i in range(devices)]
            mine = kept.reshape(groups, width, width)
            received = [permute(part, swap) for part in (mine[: groups // 2], mine[groups // 2 :])]

            def assemble(received, tier_num=tier_num, groups=groups, front_num=front_num, mine=mine):
                side_row = child_sides[tier_num]
                parent_half = (device // groups) & 1
                total = fronts[tier_num + 1].reshape(2, groups, width, width).astype(jnp.float32)
                halves = jnp.arange(2, dtype=jnp.int32)
                for part, flip in ((mine, 0), (jnp.concatenate(received, 0), 1)):
                    sides = lax.dynamic_slice_in_dim(side_row, (front_num ^ flip) * groups, groups, 0)
                    own_side = side_row[device ^ (groups * flip)]
                    keep = (sides[None, :] == halves[:, None]) & (own_side == parent_half)
                    total = total + jnp.where(
                        keep[:, :, None, None], part[None].astype(jnp.float32), 0.0
                    )
                return total.astype(jnp.bfloat16).reshape(-1, width)

            if tier_num == 0:
                column = assemble(received)
    return tuple(results)


def solution(mesh):
    across, down, whole = P(None, AXIS), P(AXIS, None), P()
    return jax.shard_map(
        shards,
        mesh=mesh,
        in_specs=(across,) * 4 + (down,) * 4 + (whole,) * 5,
        out_specs=(across,) * 4,
        check_vma=False,
    )
```

```python
import functools

import jax
import jax.numpy as jnp
from jax import lax
from jax.experimental import pallas as pl
from jax.experimental.pallas import tpu as pltpu
from jax.sharding import PartitionSpec as P

AXIS = "cube"
SHIFT = {"y": 5, "z": 3, "x": 1}


def permute(array, pairs):
    return lax.ppermute(array, AXIS, pairs)


def moved(device, axis, count, step):
    shift = SHIFT[axis]
    position = (device >> shift) & (count - 1)
    return device - (position << shift) + (((position + step) % count) << shift)


STAGES = (
    ((("z", "z"), 2), (("x", "x"), 4)),
    ((("x", "z"), 4), (("z", "x"), 4)),
    ((("y", "y"), 2), (("x", "z"), 4), (("z", "x"), 4)),
    ((("y", "y"), 4), (("x", "z"), 4), (("z", "x"), 4)),
)


def axis_position(device, axis, count):
    return (device >> SHIFT[axis]) & (count - 1)


def gather_pieces(block, axes, count):
    devices = lax.axis_size(AXIS)
    pieces = [block]
    for step in range(1, count):
        pieces.append(permute(block, [(moved(i, axes[i & 1], count, step), i) for i in range(devices)]))
    return pieces


def gather_stage(block, device, axes, count):
    pieces = gather_pieces(block, axes, count)
    position = jnp.where(
        device & 1 == 0, axis_position(device, axes[0], count), axis_position(device, axes[1], count)
    )
    placed = []
    for spot in range(count):
        which = jnp.bitwise_and(spot - position, count - 1)
        if count == 2:
            placed.append(jnp.where(which == 0, pieces[0], pieces[1]))
        else:
            placed.append(lax.select_n(which, *pieces))
    return jnp.concatenate(placed, 0)


def gather_rows(block, device, tier_num, early):
    devices = lax.axis_size(AXIS)
    stages = STAGES[tier_num]
    half = block[None]
    received = []
    for stage, (axes, count) in enumerate(stages):
        if stage == len(stages) - 1:
            if early is not None:
                half, received[0] = lax.optimization_barrier((half, received[0]))
            pieces = gather_pieces(half, axes, count)
        else:
            half = gather_stage(half, device, axes, count)
            if early is not None and stage == 0:
                swap, *parts = early
                half, *parts = lax.optimization_barrier((half, *parts))
                received = [permute(part, swap) for part in parts]
    others = [permute(piece, [(i, i ^ 1) for i in range(devices)]) for piece in pieces]
    return pieces, others, received


def place_of(tier_num, groups, r):
    places = []
    for core in range(2):
        place, scale = 0, 1
        for axes, count in STAGES[tier_num]:
            place = place + axis_position(r, axes[core], count) * scale
            scale *= count
        places.append(place + core * (groups // 2))
    return jnp.where(r & 1 == 0, places[0], places[1])


ROLE_NONE, ROLE_FIRST, ROLE_SECOND = 0, 1, 2


def tier_kernel(tier_num, groups, width, span, count, info, column_any, column_ref, *refs):
    pieces, (final_ref, kept_ref, panel, band, bands_in, sems, band_sems) = (
        refs[: 2 * count],
        refs[2 * count :],
    )
    first, second, role, core = info[0], info[1], info[2], info[3]
    place = functools.partial(place_of, tier_num, groups)
    chunk = pl.program_id(0)
    part = groups // (2 * count)
    zero = jnp.zeros((width, width), jnp.bfloat16)

    @pl.when(chunk == 0)
    def _():
        copies = []
        for side in range(2):
            holder = core if side == 0 else 1 - core
            position = jnp.where(holder == 0, info[4], info[5])
            for step in range(count):
                slot = holder * (groups // 2) + ((position + step) & (count - 1)) * part
                copies.append(
                    pltpu.make_async_copy(
                        pieces[side * count + step],
                        panel.at[pl.ds(slot, part)],
                        sems.at[side * count + step],
                    )
                )
        for which, block in ((0, first), (1, second)):
            copies.append(
                pltpu.make_async_copy(
                    column_any.at[pl.ds(pl.multiple_of(block * width, width), width)],
                    bands_in.at[which],
                    band_sems.at[which],
                )
            )
        for copy in copies:
            copy.start()
        for copy in copies:
            copy.wait()
        at_first, at_second = place(first), place(second)
        top = panel[at_first, :, width:]

        def scale_rows(i, carry):
            both = panel[pl.ds(i * span, span)].reshape(span * width, 2 * width)
            change = jnp.dot(both[:, :width], top, preferred_element_type=jnp.float32)
            fixed = (both[:, width:].astype(jnp.float32) - change).astype(jnp.bfloat16)
            panel[pl.ds(i * span, span), :, width:] = fixed.reshape(span, width, width)
            return carry

        lax.fori_loop(0, groups // span, scale_rows, 0)
        panel[at_first, :, width:] = top
        lower = bands_in[1].astype(jnp.float32) - jnp.dot(
            panel[at_second, :, :width], bands_in[0], preferred_element_type=jnp.float32
        )
        band[:width] = bands_in[0]
        band[width:] = lower.astype(jnp.bfloat16)

        @pl.when(role == ROLE_NONE)
        def _():
            panel[at_first, :, :width] = zero
            panel[at_first, :, width:] = zero
            panel[at_second, :, width:] = zero

    places = [place(chunk * span + j) for j in range(span)]

    @pl.when(role == ROLE_NONE)
    def _():
        both = jnp.concatenate([panel[at] for at in places], 0)
        update = jnp.dot(both, band[...], preferred_element_type=jnp.float32)
        value = column_ref[...].astype(jnp.float32) - update
        final_ref[...] = value
        if kept_ref is not None:
            kept_ref[...] = value.astype(jnp.bfloat16)
            for block in (first, second):

                @pl.when((block >= chunk * span) & (block < (chunk + 1) * span))
                def _():
                    spot = pl.multiple_of((block - chunk * span) * width, width)
                    kept_ref[pl.ds(spot, width)] = zero

    for j in range(span):
        rows = pl.ds(j * width, width)
        at = places[j]

        @pl.when(role == ROLE_FIRST)
        def _():
            final_ref[rows] = panel[at, :, :width].astype(jnp.float32)

        @pl.when(role == ROLE_SECOND)
        def _():
            final_ref[rows] = panel[at, :, width:].astype(jnp.float32)

    if kept_ref is not None:

        @pl.when(role != ROLE_NONE)
        def _():
            kept_ref[...] = jnp.zeros_like(kept_ref)


def eliminate(tier_num, column, pieces, others, info, keep):
    rows, width = column.shape
    groups = rows // width
    count = len(pieces)
    span = min(8, groups)
    block = pl.BlockSpec((span * width, width), lambda i, info: (i, 0))
    anywhere = pl.BlockSpec(memory_space=pl.ANY)
    body = functools.partial(tier_kernel, tier_num, groups, width, span, count)
    if not keep:
        inner = body

        def body(info, column_any, column_ref, *refs):
            at = 2 * count + 1
            inner(info, column_any, column_ref, *refs[:at], None, *refs[at:])

    out_shape = [jax.ShapeDtypeStruct((rows, width), jnp.float32)]
    if keep:
        out_shape.append(jax.ShapeDtypeStruct((rows, width), jnp.bfloat16))
    return pl.pallas_call(
        body,
        grid_spec=pltpu.PrefetchScalarGridSpec(
            num_scalar_prefetch=1,
            grid=(groups // span,),
            in_specs=[anywhere, block] + [anywhere] * (2 * count),
            out_specs=[block] * len(out_shape),
            scratch_shapes=[
                pltpu.VMEM((groups, width, 2 * width), jnp.bfloat16),
                pltpu.VMEM((2 * width, width), jnp.bfloat16),
                pltpu.VMEM((2, width, width), jnp.bfloat16),
                pltpu.SemaphoreType.DMA((2 * count,)),
                pltpu.SemaphoreType.DMA((2,)),
            ],
        ),
        out_shape=out_shape,
        compiler_params=pltpu.CompilerParams(vmem_limit_bytes=32 * 1024 * 1024),
        cost_estimate=pl.CostEstimate(
            flops=6 * rows * width * width, bytes_accessed=12 * rows * width, transcendentals=0
        ),
    )(info, column, column, *pieces, *others)


def shards(
    front_leaf,
    front_lower,
    front_upper,
    front_root,
    inv_leaf,
    inv_lower,
    inv_upper,
    inv_root,
    pivots_leaf,
    pivots_lower,
    pivots_upper,
    pivots_root,
    child_sides,
):
    fronts = (front_leaf, front_lower, front_upper, front_root)
    inverses = (inv_leaf, inv_lower, inv_upper, inv_root)
    tables = (pivots_leaf, pivots_lower, pivots_upper, pivots_root)
    device = lax.axis_index(AXIS)
    devices = lax.axis_size(AXIS)
    width = front_leaf.shape[1]
    column = front_leaf
    results = []
    zero = jnp.zeros((), jnp.bfloat16)

    def pivots_of(tier_num):
        groups = fronts[tier_num].shape[0] // width
        row = lax.dynamic_index_in_dim(tables[tier_num], device // groups, 0, keepdims=False)
        return row[0], row[1]

    def pivot_pair(block, tier_num):
        first, second = pivots_of(tier_num)
        local = device % (fronts[tier_num].shape[0] // width)
        return jnp.concatenate(
            [jnp.where(local == first, block, zero), jnp.where(local == second, block, zero)], 1
        )

    root_scaled = jnp.dot(front_root, inv_root, preferred_element_type=jnp.float32)
    root_scaled = root_scaled.astype(jnp.bfloat16).reshape(devices, width, width)
    root_parts = [root_scaled[:, : width // 2], root_scaled[:, width // 2 :]]
    root_rows = [None, None]
    sibling_scale = permute(inv_root, [(i, i ^ (devices // 2)) for i in range(devices)])

    def pivot_rows(rows, tier_num):
        return jnp.concatenate(
            [lax.dynamic_index_in_dim(rows, block, 0, keepdims=False) for block in pivots_of(tier_num)],
            1,
        )

    carried_rows = None
    for tier_num in range(4):
        groups = fronts[tier_num].shape[0] // width
        front_num = device // groups
        local = device % groups
        teams = [list(range(i, i + groups)) for i in range(0, devices, groups)]
        table = tables[tier_num]
        pivot_row = lax.dynamic_index_in_dim(table, front_num, 0, keepdims=False)
        first, second = pivot_row[0], pivot_row[1]
        is_first, is_second = local == first, local == second

        if tier_num < 3:
            scaled = jnp.dot(column, inverses[tier_num], preferred_element_type=jnp.float32)
            scaled = scaled.astype(jnp.bfloat16)
            if tier_num > 0:
                scaled, root_rows[tier_num - 1] = lax.optimization_barrier(
                    (scaled, root_rows[tier_num - 1])
                )
            rows = lax.all_to_all(
                scaled.reshape(groups, width, width), AXIS, 0, 0, axis_index_groups=teams, tiled=True
            )
            own = jnp.concatenate(
                [
                    lax.dynamic_index_in_dim(rows, first, 0, keepdims=False),
                    lax.dynamic_index_in_dim(rows, second, 0, keepdims=False),
                ],
                1,
            )
        else:
            raw = jnp.concatenate([pivot_rows(rows, tier_num) for rows in root_rows], 0)
            own = (raw.astype(jnp.float32) + carried_rows).astype(jnp.bfloat16)
        if tier_num < 3:
            pieces, others, _ = gather_rows(own, device, tier_num, None)
        else:
            pieces, others, received = gather_rows(own, device, tier_num, to_send)
            column = assemble(received)
        axes, count = STAGES[tier_num][-1]
        role = jnp.where(is_first, ROLE_FIRST, jnp.where(is_second, ROLE_SECOND, ROLE_NONE))
        info = jnp.stack(
            [
                first,
                second,
                role,
                device & 1,
                axis_position(device, axes[0], count),
                axis_position(device, axes[1], count),
            ]
        ).astype(jnp.int32)
        made = eliminate(tier_num, column, pieces, others, info, tier_num < 3)
        results.append(made[0])
        if tier_num < 3:
            kept = made[1]
            side_row = child_sides[tier_num]
            parent_half = (device // groups) & 1
            if tier_num < 2:
                kept, part = lax.optimization_barrier((kept, root_parts[tier_num]))
                root_rows[tier_num] = lax.all_to_all(part, AXIS, 0, 0, tiled=True)
            else:
                landing = jnp.where(side_row[device] == parent_half, inv_root, sibling_scale)
                grown = jnp.dot(kept, landing, preferred_element_type=jnp.float32)
                rows = lax.all_to_all(
                    grown.astype(jnp.bfloat16).reshape(groups, width, width), AXIS, 0, 0, axis_index_groups=teams, tiled=True
                )
                found = []
                for pivot in pivots_of(tier_num + 1):
                    source = pivot % groups
                    reaches = side_row[front_num * groups + source] == pivot // groups
                    block = lax.dynamic_index_in_dim(rows, source, 0, keepdims=False)
                    found.append(jnp.where(reaches, block, zero))
                found = jnp.concatenate(found, 1)
                met = permute(found, [(i, i ^ groups) for i in range(devices)])
                carried_rows = jnp.where(
                    side_row[device] == parent_half, found.astype(jnp.float32), 0.0
                ) + jnp.where(side_row[device ^ groups] == parent_half, met.astype(jnp.float32), 0.0)
            swap = [(i, i ^ groups) for i in range(devices)]
            mine = kept.reshape(groups, width, width)
            cut = groups * 3 // 8
            to_send = (swap, mine[:cut], mine[cut:])

            def assemble(received, tier_num=tier_num, groups=groups, front_num=front_num, mine=mine):
                side_row = child_sides[tier_num]
                parent_half = (device // groups) & 1
                total = fronts[tier_num + 1].reshape(2, groups, width, width).astype(jnp.float32)
                halves = jnp.arange(2, dtype=jnp.int32)
                for part, flip in ((mine, 0), (jnp.concatenate(received, 0), 1)):
                    sides = lax.dynamic_slice_in_dim(side_row, (front_num ^ flip) * groups, groups, 0)
                    own_side = side_row[device ^ (groups * flip)]
                    keep = (sides[None, :] == halves[:, None]) & (own_side == parent_half)
                    total = total + jnp.where(
                        keep[:, :, None, None], part[None].astype(jnp.float32), 0.0
                    )
                return total.astype(jnp.bfloat16).reshape(-1, width)

            if tier_num < 2:
                column = assemble([permute(mine, swap)])
    return tuple(results)


def solution(mesh):
    across, down, whole = P(None, AXIS), P(AXIS, None), P()
    return jax.shard_map(
        shards,
        mesh=mesh,
        in_specs=(across,) * 4 + (down,) * 4 + (whole,) * 5,
        out_specs=(across,) * 4,
        check_vma=False,
    )
```

```python
import functools

import jax
import jax.numpy as jnp
from jax import lax
from jax.experimental import pallas as pl
from jax.experimental.pallas import tpu as pltpu
from jax.sharding import PartitionSpec as P

AXIS = "cube"
SHIFT = {"y": 5, "z": 3, "x": 1}


def permute(array, pairs):
    return lax.ppermute(array, AXIS, pairs)


def moved(device, axis, count, step):
    shift = SHIFT[axis]
    position = (device >> shift) & (count - 1)
    return device - (position << shift) + (((position + step) % count) << shift)


STAGES = (
    ((("z", "z"), 2), (("x", "x"), 4)),
    ((("x", "z"), 4), (("z", "x"), 4)),
    ((("y", "y"), 2), (("x", "z"), 4), (("z", "x"), 4)),
    ((("y", "y"), 4), (("x", "z"), 4), (("z", "x"), 4)),
)


def axis_position(device, axis, count):
    return (device >> SHIFT[axis]) & (count - 1)


def gather_pieces(block, axes, count):
    devices = lax.axis_size(AXIS)
    pieces = [block]
    for step in range(1, count):
        pieces.append(permute(block, [(moved(i, axes[i & 1], count, step), i) for i in range(devices)]))
    return pieces


def gather_stage(block, device, axes, count):
    pieces = gather_pieces(block, axes, count)
    position = jnp.where(
        device & 1 == 0, axis_position(device, axes[0], count), axis_position(device, axes[1], count)
    )
    placed = []
    for spot in range(count):
        which = jnp.bitwise_and(spot - position, count - 1)
        if count == 2:
            placed.append(jnp.where(which == 0, pieces[0], pieces[1]))
        else:
            placed.append(lax.select_n(which, *pieces))
    return jnp.concatenate(placed, 0)


def gather_rows(block, device, tier_num, early):
    devices = lax.axis_size(AXIS)
    stages = STAGES[tier_num]
    half = block[None]
    received = []
    for stage, (axes, count) in enumerate(stages):
        if stage == len(stages) - 1:
            if early is not None:
                half, received[0] = lax.optimization_barrier((half, received[0]))
            pieces = gather_pieces(half, axes, count)
        else:
            half = gather_stage(half, device, axes, count)
            if early is not None and stage == 0:
                swap, *parts = early
                half, *parts = lax.optimization_barrier((half, *parts))
                received = [permute(part, swap) for part in parts]
    others = [permute(piece, [(i, i ^ 1) for i in range(devices)]) for piece in pieces]
    return pieces, others, received


def place_of(tier_num, groups, r):
    places = []
    for core in range(2):
        place, scale = 0, 1
        for axes, count in STAGES[tier_num]:
            place = place + axis_position(r, axes[core], count) * scale
            scale *= count
        places.append(place + core * (groups // 2))
    return jnp.where(r & 1 == 0, places[0], places[1])


ROLE_NONE, ROLE_FIRST, ROLE_SECOND = 0, 1, 2


def tier_kernel(tier_num, groups, width, span, count, info, column_any, column_ref, *refs):
    pieces, (final_ref, kept_ref, panel, band, bands_in, top_ref, lower_ref, sems, band_sems) = (
        refs[: 2 * count],
        refs[2 * count :],
    )
    first, second, role, core, *spots = [info[tier_num * 6 + i] for i in range(6)]
    place = functools.partial(place_of, tier_num, groups)
    chunk = pl.program_id(0)
    part = groups // (2 * count)
    zero = jnp.zeros((width, width), jnp.bfloat16)

    @pl.when(chunk == 0)
    def _():
        copies = []
        for side in range(2):
            holder = core if side == 0 else 1 - core
            position = jnp.where(holder == 0, spots[0], spots[1])
            for step in range(count):
                slot = holder * (groups // 2) + ((position + step) & (count - 1)) * part
                copies.append(
                    pltpu.make_async_copy(
                        pieces[side * count + step],
                        panel.at[pl.ds(slot, part)],
                        sems.at[side * count + step],
                    )
                )
        for which, block in ((0, first), (1, second)):
            copies.append(
                pltpu.make_async_copy(
                    column_any.at[pl.ds(pl.multiple_of(block * width, width), width)],
                    bands_in.at[which],
                    band_sems.at[which],
                )
            )
        for copy in copies:
            copy.start()
        for copy in copies:
            copy.wait()
        at_first, at_second = place(first), place(second)
        top = panel[at_first, :, width:]

        top_ref[...] = top
        lower = bands_in[1].astype(jnp.float32) - jnp.dot(
            panel[at_second, :, :width], bands_in[0], preferred_element_type=jnp.float32
        )
        lower_ref[...] = lower
        band[:width] = bands_in[0]
        band[width:] = lower.astype(jnp.bfloat16)

    def patch(block, ref, value):
        @pl.when((block >= chunk * span) & (block < (chunk + 1) * span))
        def _():
            rows = pl.ds(pl.multiple_of((block - chunk * span) * width, width), width)
            ref[rows] = value(rows)

    def factors():
        both = jnp.concatenate([panel[place(chunk * span + j)] for j in range(span)], 0)
        change = jnp.dot(both[:, :width], top_ref[...], preferred_element_type=jnp.float32)
        factor1 = (both[:, width:].astype(jnp.float32) - change).astype(jnp.bfloat16)
        return both[:, :width], factor1

    @pl.when(role == ROLE_NONE)
    def _():
        update = jnp.dot(
            jnp.concatenate(factors(), 1), band[...], preferred_element_type=jnp.float32
        )
        value = column_ref[...].astype(jnp.float32) - update
        final_ref[...] = value
        patch(first, final_ref, lambda rows: column_ref[rows].astype(jnp.float32))
        patch(second, final_ref, lambda rows: lower_ref[...])
        if kept_ref is not None:
            kept_ref[...] = value.astype(jnp.bfloat16)
            patch(first, kept_ref, lambda rows: zero)
            patch(second, kept_ref, lambda rows: zero)

    @pl.when(role == ROLE_FIRST)
    def _():
        for j in range(span):
            final_ref[pl.ds(j * width, width)] = panel[
                place(chunk * span + j), :, :width
            ].astype(jnp.float32)

    @pl.when(role == ROLE_SECOND)
    def _():
        final_ref[...] = factors()[1].astype(jnp.float32)
        patch(first, final_ref, lambda rows: top_ref[...].astype(jnp.float32))

    if kept_ref is not None:

        @pl.when(role != ROLE_NONE)
        def _():
            kept_ref[...] = jnp.zeros_like(kept_ref)


def eliminate(tier_num, column, pieces, others, info, keep):
    rows, width = column.shape
    groups = rows // width
    count = len(pieces)
    span = min(8, groups)
    block = pl.BlockSpec((span * width, width), lambda i, info: (i, 0))
    anywhere = pl.BlockSpec(memory_space=pl.ANY)
    body = functools.partial(tier_kernel, tier_num, groups, width, span, count)
    if not keep:
        inner = body

        def body(info, column_any, column_ref, *refs):
            at = 2 * count + 1
            inner(info, column_any, column_ref, *refs[:at], None, *refs[at:])

    out_shape = [jax.ShapeDtypeStruct((rows, width), jnp.float32)]
    if keep:
        out_shape.append(jax.ShapeDtypeStruct((rows, width), jnp.bfloat16))
    return pl.pallas_call(
        body,
        grid_spec=pltpu.PrefetchScalarGridSpec(
            num_scalar_prefetch=1,
            grid=(groups // span,),
            in_specs=[anywhere, block] + [anywhere] * (2 * count),
            out_specs=[block] * len(out_shape),
            scratch_shapes=[
                pltpu.VMEM((groups, width, 2 * width), jnp.bfloat16),
                pltpu.VMEM((2 * width, width), jnp.bfloat16),
                pltpu.VMEM((2, width, width), jnp.bfloat16),
                pltpu.VMEM((width, width), jnp.bfloat16),
                pltpu.VMEM((width, width), jnp.float32),
                pltpu.SemaphoreType.DMA((2 * count,)),
                pltpu.SemaphoreType.DMA((2,)),
            ],
        ),
        out_shape=out_shape,
        compiler_params=pltpu.CompilerParams(vmem_limit_bytes=32 * 1024 * 1024),
        cost_estimate=pl.CostEstimate(
            flops=6 * rows * width * width, bytes_accessed=12 * rows * width, transcendentals=0
        ),
    )(info, column, column, *pieces, *others)


def shards(
    front_leaf,
    front_lower,
    front_upper,
    front_root,
    inv_leaf,
    inv_lower,
    inv_upper,
    inv_root,
    pivots_leaf,
    pivots_lower,
    pivots_upper,
    pivots_root,
    child_sides,
):
    fronts = (front_leaf, front_lower, front_upper, front_root)
    inverses = (inv_leaf, inv_lower, inv_upper, inv_root)
    tables = (pivots_leaf, pivots_lower, pivots_upper, pivots_root)
    device = lax.axis_index(AXIS)
    devices = lax.axis_size(AXIS)
    width = front_leaf.shape[1]
    column = front_leaf
    results = []
    zero = jnp.zeros((), jnp.bfloat16)

    def pivots_of(tier_num):
        groups = fronts[tier_num].shape[0] // width
        row = lax.dynamic_index_in_dim(tables[tier_num], device // groups, 0, keepdims=False)
        return row[0], row[1]

    def pivot_pair(block, tier_num):
        first, second = pivots_of(tier_num)
        local = device % (fronts[tier_num].shape[0] // width)
        return jnp.concatenate(
            [jnp.where(local == first, block, zero), jnp.where(local == second, block, zero)], 1
        )

    info = []
    for tier_num in range(4):
        first, second = pivots_of(tier_num)
        local = device % (fronts[tier_num].shape[0] // width)
        role = jnp.where(local == first, ROLE_FIRST, jnp.where(local == second, ROLE_SECOND, ROLE_NONE))
        axes, count = STAGES[tier_num][-1]
        spots = [axis_position(device, axis, count) for axis in axes]
        info += [first, second, role, device & 1, *spots]
    info = jnp.stack(info).astype(jnp.int32)

    core = device & 1
    root_first, root_second = pivots_of(3)
    def spread_root(inverse):
        root_scaled = jnp.dot(front_root, inverse, preferred_element_type=jnp.float32)
        root_scaled = root_scaled.astype(jnp.bfloat16).reshape(4, 4, 4, 2, width, width)
        here = lax.dynamic_index_in_dim(root_scaled, core, 3, keepdims=False)
        there = lax.dynamic_index_in_dim(root_scaled, 1 - core, 3, keepdims=False)
        there = permute(there, [(i, i ^ 1) for i in range(devices)])
        root_block = jnp.stack(
            [jnp.where(block & 1 == core, here, there) for block in (root_first, root_second)], 3
        )
        root_block = jnp.where(core == 0, jnp.transpose(root_block, (2, 0, 1, 3, 4, 5)), root_block)
        return root_block

    def scatter_stage(block, axes, after):
        def along(index):
            return jnp.where(core == 0, axis_position(index, axes[0], 4), axis_position(index, axes[1], 4))

        position = along(device)
        sent = [
            lax.dynamic_index_in_dim(block, (position + step) & 3, 0, keepdims=False)
            for step in range(4)
        ]
        if after is not None:
            after, *sent = lax.optimization_barrier((after, *sent))
        got = [sent[0]]
        for step in range(1, 4):
            got.append(
                permute(sent[step], [(i, moved(i, axes[i & 1], 4, step)) for i in range(devices)])
            )
        panel_dim = got[0].ndim - 3
        chosen = []
        for panel, pivot in enumerate((root_first, root_second)):
            parts = [lax.index_in_dim(piece, panel, panel_dim, keepdims=False) for piece in got]
            chosen.append(lax.select_n((position - along(pivot)) & 3, *parts))
        return jnp.stack(chosen, panel_dim), after

    sibling_scale = permute(inv_root, [(i, i ^ (devices // 2)) for i in range(devices)])

    carried_rows = None
    for tier_num in range(4):
        groups = fronts[tier_num].shape[0] // width
        front_num = device // groups
        local = device % groups
        teams = [list(range(i, i + groups)) for i in range(0, devices, groups)]
        table = tables[tier_num]
        pivot_row = lax.dynamic_index_in_dim(table, front_num, 0, keepdims=False)
        first, second = pivot_row[0], pivot_row[1]
        is_first, is_second = local == first, local == second

        if tier_num < 3:
            scaled = jnp.dot(column, inverses[tier_num], preferred_element_type=jnp.float32)
            scaled = scaled.astype(jnp.bfloat16)
            if tier_num > 0:
                scaled, root_block = lax.optimization_barrier((scaled, root_block))
            rows = lax.all_to_all(
                scaled.reshape(groups, width, width), AXIS, 0, 0, axis_index_groups=teams, tiled=True
            )
            own = jnp.concatenate(
                [
                    lax.dynamic_index_in_dim(rows, first, 0, keepdims=False),
                    lax.dynamic_index_in_dim(rows, second, 0, keepdims=False),
                ],
                1,
            )
        else:
            raw = jnp.concatenate([root_block[0], root_block[1]], 1)
            own = (raw.astype(jnp.float32) + carried_rows).astype(jnp.bfloat16)
        if tier_num < 3:
            pieces, others, _ = gather_rows(own, device, tier_num, None)
            if tier_num == 0:
                pieces[1], inverse = lax.optimization_barrier((pieces[1], inv_root))
                root_block = spread_root(inverse)
        else:
            pieces, others, received = gather_rows(own, device, tier_num, to_send)
            column = assemble(received)
        made = eliminate(tier_num, column, pieces, others, info, tier_num < 3)
        results.append(made[0])
        if tier_num < 3:
            kept = made[1]
            side_row = child_sides[tier_num]
            parent_half = (device // groups) & 1
            if tier_num < 2:
                if tier_num == 0:
                    root_block, kept = scatter_stage(root_block, ("x", "y"), kept)
                else:
                    root_block, kept = scatter_stage(root_block, ("y", "z"), kept)
                    root_block, _ = scatter_stage(root_block, ("z", "x"), None)
            else:
                landing = jnp.where(side_row[device] == parent_half, inv_root, sibling_scale)
                grown = jnp.dot(kept, landing, preferred_element_type=jnp.float32)
                rows = lax.all_to_all(
                    grown.astype(jnp.bfloat16).reshape(groups, width, width), AXIS, 0, 0, axis_index_groups=teams, tiled=True
                )
                found = []
                for pivot in pivots_of(tier_num + 1):
                    source = pivot % groups
                    reaches = side_row[front_num * groups + source] == pivot // groups
                    block = lax.dynamic_index_in_dim(rows, source, 0, keepdims=False)
                    found.append(jnp.where(reaches, block, zero))
                found = jnp.concatenate(found, 1)
                met = permute(found, [(i, i ^ groups) for i in range(devices)])
                carried_rows = jnp.where(
                    side_row[device] == parent_half, found.astype(jnp.float32), 0.0
                ) + jnp.where(side_row[device ^ groups] == parent_half, met.astype(jnp.float32), 0.0)
            swap = [(i, i ^ groups) for i in range(devices)]
            mine = kept.reshape(groups, width, width)
            cut = groups * 3 // 8
            to_send = (swap, mine[:cut], mine[cut:])

            def assemble(received, tier_num=tier_num, groups=groups, front_num=front_num, mine=mine):
                side_row = child_sides[tier_num]
                parent_half = (device // groups) & 1
                total = fronts[tier_num + 1].reshape(2, groups, width, width).astype(jnp.float32)
                halves = jnp.arange(2, dtype=jnp.int32)
                for part, flip in ((mine, 0), (jnp.concatenate(received, 0), 1)):
                    sides = lax.dynamic_slice_in_dim(side_row, (front_num ^ flip) * groups, groups, 0)
                    own_side = side_row[device ^ (groups * flip)]
                    keep = (sides[None, :] == halves[:, None]) & (own_side == parent_half)
                    total = total + jnp.where(
                        keep[:, :, None, None], part[None].astype(jnp.float32), 0.0
                    )
                return total.astype(jnp.bfloat16).reshape(-1, width)

            if tier_num < 2:
                column = assemble([permute(mine, swap)])
    return tuple(results)


def solution(mesh):
    across, down, whole = P(None, AXIS), P(AXIS, None), P()
    return jax.shard_map(
        shards,
        mesh=mesh,
        in_specs=(across,) * 4 + (down,) * 4 + (whole,) * 5,
        out_specs=(across,) * 4,
        check_vma=False,
    )
```

```python
import functools

import jax
import jax.numpy as jnp
from jax import lax
from jax.experimental import pallas as pl
from jax.experimental.pallas import tpu as pltpu
from jax.sharding import PartitionSpec as P

AXIS = "cube"
SHIFT = {"y": 5, "z": 3, "x": 1}


def permute(array, pairs):
    return lax.ppermute(array, AXIS, pairs)


def moved(device, axis, count, step):
    shift = SHIFT[axis]
    position = (device >> shift) & (count - 1)
    return device - (position << shift) + (((position + step) % count) << shift)


STAGES = (
    ((("z", "z"), 2), (("x", "x"), 4)),
    ((("x", "z"), 4), (("z", "x"), 4)),
    ((("y", "y"), 2), (("x", "z"), 4), (("z", "x"), 4)),
    ((("y", "y"), 4), (("x", "z"), 4), (("z", "x"), 4)),
)


def axis_position(device, axis, count):
    return (device >> SHIFT[axis]) & (count - 1)


def gather_pieces(block, axes, count):
    devices = lax.axis_size(AXIS)
    pieces = [block]
    for step in range(1, count):
        pieces.append(permute(block, [(moved(i, axes[i & 1], count, step), i) for i in range(devices)]))
    return pieces


def gather_stage(block, device, axes, count):
    pieces = gather_pieces(block, axes, count)
    position = jnp.where(
        device & 1 == 0, axis_position(device, axes[0], count), axis_position(device, axes[1], count)
    )
    placed = []
    for spot in range(count):
        which = jnp.bitwise_and(spot - position, count - 1)
        if count == 2:
            placed.append(jnp.where(which == 0, pieces[0], pieces[1]))
        else:
            placed.append(lax.select_n(which, *pieces))
    return jnp.concatenate(placed, 0)


def gather_rows(block, device, tier_num, early):
    devices = lax.axis_size(AXIS)
    stages = STAGES[tier_num]
    half = block[None]
    received = []
    for stage, (axes, count) in enumerate(stages):
        if stage == len(stages) - 1:
            if early is not None:
                half, received[0] = lax.optimization_barrier((half, received[0]))
            pieces = gather_pieces(half, axes, count)
        else:
            half = gather_stage(half, device, axes, count)
            if early is not None and stage == 0:
                swap, *parts = early
                half, *parts = lax.optimization_barrier((half, *parts))
                received = [permute(part, swap) for part in parts]
    others = [permute(piece, [(i, i ^ 1) for i in range(devices)]) for piece in pieces]
    return pieces, others, received


def place_of(tier_num, groups, r):
    places = []
    for core in range(2):
        place, scale = 0, 1
        for axes, count in STAGES[tier_num]:
            place = place + axis_position(r, axes[core], count) * scale
            scale *= count
        places.append(place + core * (groups // 2))
    return jnp.where(r & 1 == 0, places[0], places[1])


ROLE_NONE, ROLE_FIRST, ROLE_SECOND = 0, 1, 2


def tier_kernel(tier_num, groups, width, span, count, info, column_any, column_ref, *refs):
    pieces, (final_ref, kept_ref, panel, band, bands_in, top_ref, lower_ref, sems, band_sems) = (
        refs[: 2 * count],
        refs[2 * count :],
    )
    first, second, role, core, *spots = [info[tier_num * 6 + i] for i in range(6)]
    place = functools.partial(place_of, tier_num, groups)
    chunk = pl.program_id(0)
    part = groups // (2 * count)
    zero = jnp.zeros((width, width), jnp.bfloat16)

    @pl.when(chunk == 0)
    def _():
        copies = []
        for side in range(2):
            holder = core if side == 0 else 1 - core
            position = jnp.where(holder == 0, spots[0], spots[1])
            for step in range(count):
                slot = holder * (groups // 2) + ((position + step) & (count - 1)) * part
                copies.append(
                    pltpu.make_async_copy(
                        pieces[side * count + step],
                        panel.at[pl.ds(slot, part)],
                        sems.at[side * count + step],
                    )
                )
        for which, block in ((0, first), (1, second)):
            copies.append(
                pltpu.make_async_copy(
                    column_any.at[pl.ds(pl.multiple_of(block * width, width), width)],
                    bands_in.at[which],
                    band_sems.at[which],
                )
            )
        for copy in copies:
            copy.start()
        for copy in copies:
            copy.wait()
        at_first, at_second = place(first), place(second)
        top = panel[at_first, :, width:]

        top_ref[...] = top
        lower = bands_in[1].astype(jnp.float32) - jnp.dot(
            panel[at_second, :, :width], bands_in[0], preferred_element_type=jnp.float32
        )
        lower_ref[...] = lower
        band[:width] = bands_in[0]
        band[width:] = lower.astype(jnp.bfloat16)

    def patch(block, ref, value):
        @pl.when((block >= chunk * span) & (block < (chunk + 1) * span))
        def _():
            rows = pl.ds(pl.multiple_of((block - chunk * span) * width, width), width)
            ref[rows] = value(rows)

    def factors():
        both = jnp.concatenate([panel[place(chunk * span + j)] for j in range(span)], 0)
        change = jnp.dot(both[:, :width], top_ref[...], preferred_element_type=jnp.float32)
        factor1 = (both[:, width:].astype(jnp.float32) - change).astype(jnp.bfloat16)
        return both[:, :width], factor1

    @pl.when(role == ROLE_NONE)
    def _():
        update = jnp.dot(
            jnp.concatenate(factors(), 1), band[...], preferred_element_type=jnp.float32
        )
        value = column_ref[...].astype(jnp.float32) - update
        final_ref[...] = value
        patch(first, final_ref, lambda rows: column_ref[rows].astype(jnp.float32))
        patch(second, final_ref, lambda rows: lower_ref[...])
        if kept_ref is not None:
            kept_ref[...] = value.astype(jnp.bfloat16)
            patch(first, kept_ref, lambda rows: zero)
            patch(second, kept_ref, lambda rows: zero)

    @pl.when(role == ROLE_FIRST)
    def _():
        for j in range(span):
            final_ref[pl.ds(j * width, width)] = panel[
                place(chunk * span + j), :, :width
            ].astype(jnp.float32)

    @pl.when(role == ROLE_SECOND)
    def _():
        final_ref[...] = factors()[1].astype(jnp.float32)
        patch(first, final_ref, lambda rows: top_ref[...].astype(jnp.float32))

    if kept_ref is not None:

        @pl.when(role != ROLE_NONE)
        def _():
            kept_ref[...] = jnp.zeros_like(kept_ref)


def eliminate(tier_num, column, pieces, others, info, keep):
    rows, width = column.shape
    groups = rows // width
    count = len(pieces)
    span = min(8, groups)
    block = pl.BlockSpec((span * width, width), lambda i, info: (i, 0))
    anywhere = pl.BlockSpec(memory_space=pl.ANY)
    body = functools.partial(tier_kernel, tier_num, groups, width, span, count)
    if not keep:
        inner = body

        def body(info, column_any, column_ref, *refs):
            at = 2 * count + 1
            inner(info, column_any, column_ref, *refs[:at], None, *refs[at:])

    out_shape = [jax.ShapeDtypeStruct((rows, width), jnp.float32)]
    if keep:
        out_shape.append(jax.ShapeDtypeStruct((rows, width), jnp.bfloat16))
    return pl.pallas_call(
        body,
        grid_spec=pltpu.PrefetchScalarGridSpec(
            num_scalar_prefetch=1,
            grid=(groups // span,),
            in_specs=[anywhere, block] + [anywhere] * (2 * count),
            out_specs=[block] * len(out_shape),
            scratch_shapes=[
                pltpu.VMEM((groups, width, 2 * width), jnp.bfloat16),
                pltpu.VMEM((2 * width, width), jnp.bfloat16),
                pltpu.VMEM((2, width, width), jnp.bfloat16),
                pltpu.VMEM((width, width), jnp.bfloat16),
                pltpu.VMEM((width, width), jnp.float32),
                pltpu.SemaphoreType.DMA((2 * count,)),
                pltpu.SemaphoreType.DMA((2,)),
            ],
        ),
        out_shape=out_shape,
        compiler_params=pltpu.CompilerParams(vmem_limit_bytes=32 * 1024 * 1024),
        cost_estimate=pl.CostEstimate(
            flops=6 * rows * width * width, bytes_accessed=12 * rows * width, transcendentals=0
        ),
    )(info, column, column, *pieces, *others)


def shards(
    front_leaf,
    front_lower,
    front_upper,
    front_root,
    inv_leaf,
    inv_lower,
    inv_upper,
    inv_root,
    pivots_leaf,
    pivots_lower,
    pivots_upper,
    pivots_root,
    child_sides,
):
    fronts = (front_leaf, front_lower, front_upper, front_root)
    inverses = (inv_leaf, inv_lower, inv_upper, inv_root)
    tables = (pivots_leaf, pivots_lower, pivots_upper, pivots_root)
    device = lax.axis_index(AXIS)
    devices = lax.axis_size(AXIS)
    width = front_leaf.shape[1]
    column = front_leaf
    results = []
    zero = jnp.zeros((), jnp.bfloat16)

    def pivots_of(tier_num):
        groups = fronts[tier_num].shape[0] // width
        row = lax.dynamic_index_in_dim(tables[tier_num], device // groups, 0, keepdims=False)
        return row[0], row[1]

    def pivot_pair(block, tier_num):
        first, second = pivots_of(tier_num)
        local = device % (fronts[tier_num].shape[0] // width)
        return jnp.concatenate(
            [jnp.where(local == first, block, zero), jnp.where(local == second, block, zero)], 1
        )

    info = []
    for tier_num in range(4):
        first, second = pivots_of(tier_num)
        local = device % (fronts[tier_num].shape[0] // width)
        role = jnp.where(local == first, ROLE_FIRST, jnp.where(local == second, ROLE_SECOND, ROLE_NONE))
        axes, count = STAGES[tier_num][-1]
        spots = [axis_position(device, axis, count) for axis in axes]
        info += [first, second, role, device & 1, *spots]
    info = jnp.stack(info).astype(jnp.int32)

    core = device & 1
    root_first, root_second = pivots_of(3)

    def spread_root(inverse):
        root_scaled = jnp.dot(front_root, inverse, preferred_element_type=jnp.float32)
        root_scaled = root_scaled.astype(jnp.bfloat16).reshape(4, 4, 4, 2, width, width)
        here = lax.dynamic_index_in_dim(root_scaled, core, 3, keepdims=False)
        there = lax.dynamic_index_in_dim(root_scaled, 1 - core, 3, keepdims=False)
        there = permute(there, [(i, i ^ 1) for i in range(devices)])
        root_block = jnp.stack(
            [jnp.where(block & 1 == core, here, there) for block in (root_first, root_second)], 3
        )
        root_block = jnp.where(core == 0, jnp.transpose(root_block, (2, 0, 1, 3, 4, 5)), root_block)
        return root_block

    def scatter_stage(block, axes, after):
        def along(index):
            return jnp.where(core == 0, axis_position(index, axes[0], 4), axis_position(index, axes[1], 4))

        position = along(device)
        sent = [
            lax.dynamic_index_in_dim(block, (position + step) & 3, 0, keepdims=False)
            for step in range(4)
        ]
        if after is not None:
            after, *sent = lax.optimization_barrier((after, *sent))
        got = [sent[0]]
        for step in range(1, 4):
            got.append(
                permute(sent[step], [(i, moved(i, axes[i & 1], 4, step)) for i in range(devices)])
            )
        panel_dim = got[0].ndim - 3
        chosen = []
        for panel, pivot in enumerate((root_first, root_second)):
            parts = [lax.index_in_dim(piece, panel, panel_dim, keepdims=False) for piece in got]
            chosen.append(lax.select_n((position - along(pivot)) & 3, *parts))
        return jnp.stack(chosen, panel_dim), after

    root_block = spread_root(inv_root)
    sibling_scale = permute(inv_root, [(i, i ^ (devices // 2)) for i in range(devices)])

    carried_rows = None
    for tier_num in range(4):
        groups = fronts[tier_num].shape[0] // width
        front_num = device // groups
        local = device % groups
        teams = [list(range(i, i + groups)) for i in range(0, devices, groups)]
        table = tables[tier_num]
        pivot_row = lax.dynamic_index_in_dim(table, front_num, 0, keepdims=False)
        first, second = pivot_row[0], pivot_row[1]
        is_first, is_second = local == first, local == second

        if tier_num < 3:
            scaled = jnp.dot(column, inverses[tier_num], preferred_element_type=jnp.float32)
            scaled = scaled.astype(jnp.bfloat16)
            if tier_num > 0:
                scaled, root_block = lax.optimization_barrier((scaled, root_block))
            rows = lax.all_to_all(
                scaled.reshape(groups, width, width), AXIS, 0, 0, axis_index_groups=teams, tiled=True
            )
            own = jnp.concatenate(
                [
                    lax.dynamic_index_in_dim(rows, first, 0, keepdims=False),
                    lax.dynamic_index_in_dim(rows, second, 0, keepdims=False),
                ],
                1,
            )
        else:
            raw = jnp.concatenate([root_block[0], root_block[1]], 1)
            own = (raw.astype(jnp.float32) + carried_rows).astype(jnp.bfloat16)
        if tier_num < 3:
            pieces, others, _ = gather_rows(own, device, tier_num, None)
        else:
            pieces, others, received = gather_rows(own, device, tier_num, to_send)
            column = assemble(received)
        made = eliminate(tier_num, column, pieces, others, info, tier_num < 3)
        results.append(made[0])
        if tier_num < 3:
            kept = made[1]
            side_row = child_sides[tier_num]
            parent_half = (device // groups) & 1
            if tier_num < 2:
                if tier_num == 0:
                    root_block, kept = scatter_stage(root_block, ("x", "y"), kept)
                else:
                    root_block, kept = scatter_stage(root_block, ("y", "z"), kept)
                    root_block, _ = scatter_stage(root_block, ("z", "x"), None)
            else:
                landing = jnp.where(side_row[device] == parent_half, inv_root, sibling_scale)
                grown = jnp.dot(kept, landing, preferred_element_type=jnp.float32)
                rows = lax.all_to_all(
                    grown.astype(jnp.bfloat16).reshape(groups, width, width), AXIS, 0, 0, axis_index_groups=teams, tiled=True
                )
                found = []
                for pivot in pivots_of(tier_num + 1):
                    source = pivot % groups
                    reaches = side_row[front_num * groups + source] == pivot // groups
                    block = lax.dynamic_index_in_dim(rows, source, 0, keepdims=False)
                    found.append(jnp.where(reaches, block, zero))
                found = jnp.concatenate(found, 1)
                met = permute(found, [(i, i ^ groups) for i in range(devices)])
                carried_rows = jnp.where(
                    side_row[device] == parent_half, found.astype(jnp.float32), 0.0
                ) + jnp.where(side_row[device ^ groups] == parent_half, met.astype(jnp.float32), 0.0)
            swap = [(i, i ^ groups) for i in range(devices)]
            mine = kept.reshape(groups, width, width)
            cut = groups * 3 // 8
            to_send = (swap, mine[:cut], mine[cut:])

            def assemble(received, tier_num=tier_num, groups=groups, front_num=front_num, mine=mine):
                side_row = child_sides[tier_num]
                parent_half = (device // groups) & 1
                total = fronts[tier_num + 1].reshape(2, groups, width, width).astype(jnp.float32)
                halves = jnp.arange(2, dtype=jnp.int32)
                for part, flip in ((mine, 0), (jnp.concatenate(received, 0), 1)):
                    sides = lax.dynamic_slice_in_dim(side_row, (front_num ^ flip) * groups, groups, 0)
                    own_side = side_row[device ^ (groups * flip)]
                    keep = (sides[None, :] == halves[:, None]) & (own_side == parent_half)
                    total = total + jnp.where(
                        keep[:, :, None, None], part[None].astype(jnp.float32), 0.0
                    )
                return total.astype(jnp.bfloat16).reshape(-1, width)

            if tier_num < 2:
                column = assemble([permute(mine, swap)])
    return tuple(results)


def solution(mesh):
    across, down, whole = P(None, AXIS), P(AXIS, None), P()
    return jax.shard_map(
        shards,
        mesh=mesh,
        in_specs=(across,) * 4 + (down,) * 4 + (whole,) * 5,
        out_specs=(across,) * 4,
        check_vma=False,
    )
```

```python
import functools

import jax
import jax.numpy as jnp
from jax import lax
from jax.experimental import pallas as pl
from jax.experimental.pallas import tpu as pltpu
from jax.sharding import PartitionSpec as P

AXIS = "cube"
SHIFT = {"y": 5, "z": 3, "x": 1}


def permute(array, pairs):
    return lax.ppermute(array, AXIS, pairs)


def moved(device, axis, count, step):
    shift = SHIFT[axis]
    position = (device >> shift) & (count - 1)
    return device - (position << shift) + (((position + step) % count) << shift)


STAGES = (
    ((("z", "z"), 2), (("x", "x"), 4)),
    ((("x", "z"), 4), (("z", "x"), 4)),
    ((("y", "y"), 2), (("x", "z"), 4), (("z", "x"), 4)),
    ((("y", "y"), 4), (("x", "z"), 4), (("z", "x"), 4)),
)


def axis_position(device, axis, count):
    return (device >> SHIFT[axis]) & (count - 1)


def gather_pieces(block, axes, count):
    devices = lax.axis_size(AXIS)
    pieces = [block]
    for step in range(1, count):
        pieces.append(permute(block, [(moved(i, axes[i & 1], count, step), i) for i in range(devices)]))
    return pieces


def gather_stage(block, device, axes, count):
    pieces = gather_pieces(block, axes, count)
    position = jnp.where(
        device & 1 == 0, axis_position(device, axes[0], count), axis_position(device, axes[1], count)
    )
    placed = []
    for spot in range(count):
        which = jnp.bitwise_and(spot - position, count - 1)
        if count == 2:
            placed.append(jnp.where(which == 0, pieces[0], pieces[1]))
        else:
            placed.append(lax.select_n(which, *pieces))
    return jnp.concatenate(placed, 0)


def gather_rows(block, device, tier_num, early):
    devices = lax.axis_size(AXIS)
    stages = STAGES[tier_num]
    half = block[None]
    received = []
    for stage, (axes, count) in enumerate(stages):
        if stage == len(stages) - 1:
            if early is not None:
                half, received[0] = lax.optimization_barrier((half, received[0]))
            pieces = gather_pieces(half, axes, count)
        else:
            half = gather_stage(half, device, axes, count)
            if early is not None and stage == 0:
                swap, *parts = early
                half, *parts = lax.optimization_barrier((half, *parts))
                received = [permute(part, swap) for part in parts]
    others = [permute(piece, [(i, i ^ 1) for i in range(devices)]) for piece in pieces]
    return pieces, others, received


def place_of(tier_num, groups, r):
    places = []
    for core in range(2):
        place, scale = 0, 1
        for axes, count in STAGES[tier_num]:
            place = place + axis_position(r, axes[core], count) * scale
            scale *= count
        places.append(place + core * (groups // 2))
    return jnp.where(r & 1 == 0, places[0], places[1])


ROLE_NONE, ROLE_FIRST, ROLE_SECOND = 0, 1, 2


def tier_kernel(tier_num, groups, width, span, count, info, column_any, column_ref, *refs):
    pieces, (final_ref, kept_ref, panel, band, bands_in, top_ref, lower_ref, sems, band_sems) = (
        refs[: 2 * count],
        refs[2 * count :],
    )
    first, second, role, core, *spots = [info[i] for i in range(6)]
    place = functools.partial(place_of, tier_num, groups)
    chunk = pl.program_id(0)
    part = groups // (2 * count)
    zero = jnp.zeros((width, width), jnp.bfloat16)

    @pl.when(chunk == 0)
    def _():
        copies = []
        for side in range(2):
            holder = core if side == 0 else 1 - core
            position = jnp.where(holder == 0, spots[0], spots[1])
            for step in range(count):
                slot = holder * (groups // 2) + ((position + step) & (count - 1)) * part
                copies.append(
                    pltpu.make_async_copy(
                        pieces[side * count + step],
                        panel.at[pl.ds(slot, part)],
                        sems.at[side * count + step],
                    )
                )
        for which, block in ((0, first), (1, second)):
            copies.append(
                pltpu.make_async_copy(
                    column_any.at[pl.ds(pl.multiple_of(block * width, width), width)],
                    bands_in.at[which],
                    band_sems.at[which],
                )
            )
        for copy in copies:
            copy.start()
        for copy in copies:
            copy.wait()
        at_first, at_second = place(first), place(second)
        top = panel[at_first, :, width:]

        top_ref[...] = top
        lower = bands_in[1].astype(jnp.float32) - jnp.dot(
            panel[at_second, :, :width], bands_in[0], preferred_element_type=jnp.float32
        )
        lower_ref[...] = lower
        band[:width] = bands_in[0]
        band[width:] = lower.astype(jnp.bfloat16)

    def patch(block, ref, value):
        @pl.when((block >= chunk * span) & (block < (chunk + 1) * span))
        def _():
            rows = pl.ds(pl.multiple_of((block - chunk * span) * width, width), width)
            ref[rows] = value(rows)

    def factors():
        both = jnp.concatenate([panel[place(chunk * span + j)] for j in range(span)], 0)
        change = jnp.dot(both[:, :width], top_ref[...], preferred_element_type=jnp.float32)
        factor1 = (both[:, width:].astype(jnp.float32) - change).astype(jnp.bfloat16)
        return both[:, :width], factor1

    @pl.when(role == ROLE_NONE)
    def _():
        update = jnp.dot(
            jnp.concatenate(factors(), 1), band[...], preferred_element_type=jnp.float32
        )
        value = column_ref[...].astype(jnp.float32) - update
        final_ref[...] = value
        patch(first, final_ref, lambda rows: column_ref[rows].astype(jnp.float32))
        patch(second, final_ref, lambda rows: lower_ref[...])
        if kept_ref is not None:
            kept_ref[...] = value.astype(jnp.bfloat16)
            patch(first, kept_ref, lambda rows: zero)
            patch(second, kept_ref, lambda rows: zero)

    @pl.when(role == ROLE_FIRST)
    def _():
        for j in range(span):
            final_ref[pl.ds(j * width, width)] = panel[
                place(chunk * span + j), :, :width
            ].astype(jnp.float32)

    @pl.when(role == ROLE_SECOND)
    def _():
        final_ref[...] = factors()[1].astype(jnp.float32)
        patch(first, final_ref, lambda rows: top_ref[...].astype(jnp.float32))

    if kept_ref is not None:

        @pl.when(role != ROLE_NONE)
        def _():
            kept_ref[...] = jnp.zeros_like(kept_ref)


def eliminate(tier_num, column, pieces, others, info, keep):
    rows, width = column.shape
    groups = rows // width
    count = len(pieces)
    span = min(8, groups)
    block = pl.BlockSpec((span * width, width), lambda i, info: (i, 0))
    anywhere = pl.BlockSpec(memory_space=pl.ANY)
    body = functools.partial(tier_kernel, tier_num, groups, width, span, count)
    if not keep:
        inner = body

        def body(info, column_any, column_ref, *refs):
            at = 2 * count + 1
            inner(info, column_any, column_ref, *refs[:at], None, *refs[at:])

    out_shape = [jax.ShapeDtypeStruct((rows, width), jnp.float32)]
    if keep:
        out_shape.append(jax.ShapeDtypeStruct((rows, width), jnp.bfloat16))
    return pl.pallas_call(
        body,
        grid_spec=pltpu.PrefetchScalarGridSpec(
            num_scalar_prefetch=1,
            grid=(groups // span,),
            in_specs=[anywhere, block] + [anywhere] * (2 * count),
            out_specs=[block] * len(out_shape),
            scratch_shapes=[
                pltpu.VMEM((groups, width, 2 * width), jnp.bfloat16),
                pltpu.VMEM((2 * width, width), jnp.bfloat16),
                pltpu.VMEM((2, width, width), jnp.bfloat16),
                pltpu.VMEM((width, width), jnp.bfloat16),
                pltpu.VMEM((width, width), jnp.float32),
                pltpu.SemaphoreType.DMA((2 * count,)),
                pltpu.SemaphoreType.DMA((2,)),
            ],
        ),
        out_shape=out_shape,
        compiler_params=pltpu.CompilerParams(vmem_limit_bytes=32 * 1024 * 1024),
        cost_estimate=pl.CostEstimate(
            flops=6 * rows * width * width, bytes_accessed=12 * rows * width, transcendentals=0
        ),
    )(info, column, column, *pieces, *others)


def shards(
    front_leaf,
    front_lower,
    front_upper,
    front_root,
    inv_leaf,
    inv_lower,
    inv_upper,
    inv_root,
    pivots_leaf,
    pivots_lower,
    pivots_upper,
    pivots_root,
    child_sides,
):
    fronts = (front_leaf, front_lower, front_upper, front_root)
    inverses = (inv_leaf, inv_lower, inv_upper, inv_root)
    tables = (pivots_leaf, pivots_lower, pivots_upper, pivots_root)
    device = lax.axis_index(AXIS)
    devices = lax.axis_size(AXIS)
    width = front_leaf.shape[1]
    column = front_leaf
    results = []
    zero = jnp.zeros((), jnp.bfloat16)

    def pivots_of(tier_num):
        groups = fronts[tier_num].shape[0] // width
        row = lax.dynamic_index_in_dim(tables[tier_num], device // groups, 0, keepdims=False)
        return row[0], row[1]

    def pivot_pair(block, tier_num):
        first, second = pivots_of(tier_num)
        local = device % (fronts[tier_num].shape[0] // width)
        return jnp.concatenate(
            [jnp.where(local == first, block, zero), jnp.where(local == second, block, zero)], 1
        )

    core = device & 1
    root_first, root_second = pivots_of(3)

    def spread_root(inverse):
        root_scaled = jnp.dot(front_root, inverse, preferred_element_type=jnp.float32)
        root_scaled = root_scaled.astype(jnp.bfloat16).reshape(4, 4, 4, 2, width, width)
        here = lax.dynamic_index_in_dim(root_scaled, core, 3, keepdims=False)
        there = lax.dynamic_index_in_dim(root_scaled, 1 - core, 3, keepdims=False)
        there = permute(there, [(i, i ^ 1) for i in range(devices)])
        root_block = jnp.stack(
            [jnp.where(block & 1 == core, here, there) for block in (root_first, root_second)], 3
        )
        root_block = jnp.where(core == 0, jnp.transpose(root_block, (2, 0, 1, 3, 4, 5)), root_block)
        return root_block

    def scatter_stage(block, axes, after):
        def along(index):
            return jnp.where(core == 0, axis_position(index, axes[0], 4), axis_position(index, axes[1], 4))

        position = along(device)
        sent = [
            lax.dynamic_index_in_dim(block, (position + step) & 3, 0, keepdims=False)
            for step in range(4)
        ]
        if after is not None:
            after, *sent = lax.optimization_barrier((after, *sent))
        got = [sent[0]]
        for step in range(1, 4):
            got.append(
                permute(sent[step], [(i, moved(i, axes[i & 1], 4, step)) for i in range(devices)])
            )
        panel_dim = got[0].ndim - 3
        chosen = []
        for panel, pivot in enumerate((root_first, root_second)):
            parts = [lax.index_in_dim(piece, panel, panel_dim, keepdims=False) for piece in got]
            chosen.append(lax.select_n((position - along(pivot)) & 3, *parts))
        return jnp.stack(chosen, panel_dim), after

    root_block = spread_root(inv_root)
    sibling_scale = permute(inv_root, [(i, i ^ (devices // 2)) for i in range(devices)])

    carried_rows = None
    for tier_num in range(4):
        groups = fronts[tier_num].shape[0] // width
        front_num = device // groups
        local = device % groups
        teams = [list(range(i, i + groups)) for i in range(0, devices, groups)]
        table = tables[tier_num]
        pivot_row = lax.dynamic_index_in_dim(table, front_num, 0, keepdims=False)
        first, second = pivot_row[0], pivot_row[1]
        is_first, is_second = local == first, local == second

        if tier_num < 3:
            scaled = jnp.dot(column, inverses[tier_num], preferred_element_type=jnp.float32)
            scaled = scaled.astype(jnp.bfloat16)
            if tier_num > 0:
                scaled, root_block = lax.optimization_barrier((scaled, root_block))
            rows = lax.all_to_all(
                scaled.reshape(groups, width, width), AXIS, 0, 0, axis_index_groups=teams, tiled=True
            )
            own = jnp.concatenate(
                [
                    lax.dynamic_index_in_dim(rows, first, 0, keepdims=False),
                    lax.dynamic_index_in_dim(rows, second, 0, keepdims=False),
                ],
                1,
            )
        else:
            raw = jnp.concatenate([root_block[0], root_block[1]], 1)
            own = (raw.astype(jnp.float32) + carried_rows).astype(jnp.bfloat16)
        if tier_num < 3:
            pieces, others, _ = gather_rows(own, device, tier_num, None)
        else:
            pieces, others, received = gather_rows(own, device, tier_num, to_send)
            column = assemble(received)
        axes, count = STAGES[tier_num][-1]
        role = jnp.where(is_first, ROLE_FIRST, jnp.where(is_second, ROLE_SECOND, ROLE_NONE))
        spots = [axis_position(device, axis, count) for axis in axes]
        info = jnp.stack([first, second, role, device & 1, *spots]).astype(jnp.int32)
        made = eliminate(tier_num, column, pieces, others, info, tier_num < 3)
        results.append(made[0])
        if tier_num < 3:
            kept = made[1]
            side_row = child_sides[tier_num]
            parent_half = (device // groups) & 1
            if tier_num < 2:
                if tier_num == 0:
                    root_block, kept = scatter_stage(root_block, ("x", "y"), kept)
                else:
                    root_block, kept = scatter_stage(root_block, ("y", "z"), kept)
                    root_block, _ = scatter_stage(root_block, ("z", "x"), None)
            else:
                landing = jnp.where(side_row[device] == parent_half, inv_root, sibling_scale)
                grown = jnp.dot(kept, landing, preferred_element_type=jnp.float32)
                rows = lax.all_to_all(
                    grown.astype(jnp.bfloat16).reshape(groups, width, width), AXIS, 0, 0, axis_index_groups=teams, tiled=True
                )
                found = []
                for pivot in pivots_of(tier_num + 1):
                    source = pivot % groups
                    reaches = side_row[front_num * groups + source] == pivot // groups
                    block = lax.dynamic_index_in_dim(rows, source, 0, keepdims=False)
                    found.append(jnp.where(reaches, block, zero))
                found = jnp.concatenate(found, 1)
                met = permute(found, [(i, i ^ groups) for i in range(devices)])
                carried_rows = jnp.where(
                    side_row[device] == parent_half, found.astype(jnp.float32), 0.0
                ) + jnp.where(side_row[device ^ groups] == parent_half, met.astype(jnp.float32), 0.0)
            swap = [(i, i ^ groups) for i in range(devices)]
            mine = kept.reshape(groups, width, width)
            cut = groups * 3 // 8
            to_send = (swap, mine[:cut], mine[cut:])

            def assemble(received, tier_num=tier_num, groups=groups, front_num=front_num, mine=mine):
                side_row = child_sides[tier_num]
                parent_half = (device // groups) & 1
                total = fronts[tier_num + 1].reshape(2, groups, width, width).astype(jnp.float32)
                halves = jnp.arange(2, dtype=jnp.int32)
                for part, flip in ((mine, 0), (jnp.concatenate(received, 0), 1)):
                    sides = lax.dynamic_slice_in_dim(side_row, (front_num ^ flip) * groups, groups, 0)
                    own_side = side_row[device ^ (groups * flip)]
                    keep = (sides[None, :] == halves[:, None]) & (own_side == parent_half)
                    total = total + jnp.where(
                        keep[:, :, None, None], part[None].astype(jnp.float32), 0.0
                    )
                return total.astype(jnp.bfloat16).reshape(-1, width)

            if tier_num < 2:
                column = assemble([permute(mine, swap)])
    return tuple(results)


def solution(mesh):
    across, down, whole = P(None, AXIS), P(AXIS, None), P()
    return jax.shard_map(
        shards,
        mesh=mesh,
        in_specs=(across,) * 4 + (down,) * 4 + (whole,) * 5,
        out_specs=(across,) * 4,
        check_vma=False,
    )
```
